256 devices in a mesh: dp: 8 (over y, x_hi), shard: 32 (over x_lo, z, core).
Axes of the slice: x: 4 (x_hi: 2, x_lo: 2; x = x_hi * 2 + x_lo), y: 4, z: 8, core: 2. Of those that a mesh axis runs over, the one named last changes fastest.
Arguments:
- tokens: bfloat16 [8192, 2560], P('dp'), may hold values from -6 to 6
- masters: float32 [8, 1600, 5120], P('dp', 'shard'), may hold values from -0.125 to 0.125
- cotangent: bfloat16 [8192, 12800], P('dp', 'shard'), may hold values from -6 to 6
- partner: int32 [31, 32], replicated, may hold values from 0 to 31, as said below
- slots: int32 [31, 32], replicated, may hold values from 0 to 49, as said below
Outputs:
- masters_new: float32 [8, 1600, 5120], P('dp', 'shard')
- hidden: bfloat16 [8192, 12800], P('dp', 'shard')
- input_grad: bfloat16 [8192, 2560], P(('dp', 'shard'))
- master_grads: float32 [8, 1600, 5120], P('dp', 'shard')
The draws below stay inside these ranges and needn't reach their ends.
Inputs may be any that keep to these rules, and one draw needn't show every extreme that they name: In every round partner is an involution without fixed points: partner[r, partner[r, s]] = s and partner[r, s] != s. Over the 31 rounds every shard index meets every other exactly once. The 31 slots of one shard index are distinct.
All inputs are finite; a program needn't handle non-finite values.
Results may differ from the reference program's by a relative error of at most 0.0066.
Values may be sent and summed in bfloat16 or wider, within the bound.
A program may use at most 192 MiB of HBM per device.

```python
import math
import jax
import jax.numpy as jnp
from jax import lax

D = 2560
FF = 12800
TOK_DEV = 1024
ROUNDS = 31
PAGES_DEV = 50
TOKENS = 8192
N_DP = 8
N_SHARD = 32


def bring_front(order, value):
    where = jnp.argmax(order == value)
    first = order[0]
    return order.at[where].set(first).at[0].set(value)


def draw_partner(key, part):
    key = jax.random.fold_in(key, 11)
    key_label, key_order = jax.random.split(key)
    count = N_SHARD - 1
    rounds = jnp.arange(count, dtype=jnp.int32)[:, None]
    seats = jnp.arange(N_SHARD, dtype=jnp.int32)[None, :]
    mirror = (2 * rounds - seats) % count
    base = jnp.where(seats == count, rounds + 0 * seats, jnp.where(mirror == seats, count, mirror))
    label = jax.random.permutation(key_label, N_SHARD).astype(jnp.int32)
    placed = jnp.zeros((count, N_SHARD), jnp.int32).at[:, label].set(label[base])
    order = jax.random.permutation(key_order, count)
    return placed[order].astype(jnp.int32)


def draw_slots(key, part):
    key = jax.random.fold_in(key, 12)
    keys = jax.random.split(key, N_SHARD)
    full = jax.vmap(lambda one: jax.random.permutation(one, PAGES_DEV))(keys).astype(jnp.int32)
    full = full.at[0].set(bring_front(full[0], PAGES_DEV - 1))
    full = full.at[1].set(bring_front(full[1], 0))
    return full[:, :ROUNDS].T.astype(jnp.int32)


def shard_levels(rng, dims, pieces, low, top_value):
    def one(axis_at, parts):
        heights = jax.random.uniform(jax.random.fold_in(jax.random.fold_in(rng, 6), axis_at), (parts,), jnp.float32, low / len(pieces), top_value / len(pieces))
        return jnp.repeat(jnp.exp(heights), dims[axis_at] // parts).reshape((-1,) + (1,) * (len(dims) - axis_at - 1))

    factor_of = one(*pieces[0])
    for cut in pieces[1:]:
        factor_of = factor_of * one(*cut)
    return factor_of


def gaussian(stream_key, extent, spread, most, cuts=(), kind=jnp.bfloat16):
    array = spread * jax.random.normal(stream_key, extent, jnp.float32)
    if cuts:
        array = array * shard_levels(stream_key, extent, cuts, -0.22, 0.18)
    return jnp.clip(array, -most, most).astype(kind)


def setup_inputs(seed: int = 0) -> dict:
    seeds = jax.random.split(jax.random.key(seed), 6)
    tokens = gaussian(seeds[0], (TOKENS, D), 1.0, 6.0, ((0, 8),))
    masters = gaussian(seeds[1], (N_DP, N_SHARD * PAGES_DEV, 2 * D), D ** -0.5, 0.125, ((0, 8), (1, 32)), jnp.float32)
    cotangent = gaussian(seeds[2], (TOKENS, FF), 1.0, 6.0, ((0, 8), (1, 32)))
    partner = draw_partner(jax.random.fold_in(seeds[5], 71), 0)
    slots = draw_slots(jax.random.fold_in(seeds[5], 71), 0)
    return dict(tokens=tokens, masters=masters, cotangent=cotangent, partner=partner, slots=slots)


def reference(tokens, masters, cotangent, partner, slots):
    shard_ids = jnp.arange(N_SHARD, dtype=jnp.int32)
    anchor = jnp.arange(N_SHARD * PAGES_DEV, dtype=jnp.int32).reshape(N_SHARD, PAGES_DEV)
    for step in range(ROUNDS):
        source = partner[step].astype(jnp.int32)
        taken = anchor[source, slots[step][source].astype(jnp.int32)]
        anchor = anchor.at[shard_ids, slots[step].astype(jnp.int32)].set(taken)
    masters_new = masters[:, anchor.reshape(-1)]
    arranged = masters_new.reshape(N_DP, N_SHARD, PAGES_DEV, 2 * D).transpose(1, 0, 2, 3).reshape(FF, 2 * D)
    weights = arranged.astype(jnp.bfloat16)
    gate_w = weights[:, :D]
    up_w = weights[:, D:]
    gate = jnp.dot(tokens, gate_w.T, preferred_element_type=jnp.float32)
    up = jnp.dot(tokens, up_w.T, preferred_element_type=jnp.float32)
    sig = jax.nn.sigmoid(gate)
    active = gate * sig
    hidden = (active * up).astype(jnp.bfloat16)
    grad_in = cotangent.astype(jnp.float32)
    d_gate = (grad_in * up * sig * (1.0 + gate * (1.0 - sig))).astype(jnp.bfloat16)
    d_up = (grad_in * active).astype(jnp.bfloat16)
    input_grad = (jnp.dot(d_gate, gate_w, preferred_element_type=jnp.float32) + jnp.dot(d_up, up_w, preferred_element_type=jnp.float32)).astype(jnp.bfloat16)

    def add_group(total, group):
        rows, gate_rows, up_rows = group
        part = jnp.concatenate((jnp.dot(gate_rows.T, rows, preferred_element_type=jnp.float32), jnp.dot(up_rows.T, rows, preferred_element_type=jnp.float32)), axis=1)
        return (total + part, None)
    total, unused = lax.scan(add_group, jnp.zeros((FF, 2 * D), jnp.float32), (tokens.reshape(N_DP, TOK_DEV, D), d_gate.reshape(N_DP, TOK_DEV, FF), d_up.reshape(N_DP, TOK_DEV, FF)))
    total = total * (1.0 / math.sqrt(TOKENS))
    master_grads = total.reshape(N_SHARD, N_DP, PAGES_DEV, 2 * D).transpose(1, 0, 2, 3).reshape(N_DP, N_SHARD * PAGES_DEV, 2 * D)
    return (masters_new, hidden, input_grad, master_grads)
```

```python
import functools
import math

import jax
import jax.numpy as jnp
from jax import lax
from jax.experimental import pallas as pl
from jax.experimental.pallas import tpu as pltpu
from jax.sharding import PartitionSpec as P

MESH = pl.DeviceIdType.MESH
F32, BF16 = jnp.float32, jnp.bfloat16

NY, NXH, NXL, NZ, NC = 4, 2, 2, 8, 2
SHARDS = NXL * NZ * NC
PAGES = 50
D = 2560
TOK = 1024
HALF = D // 2
QUART = D // 4
MAIN = 48
TILE = 16
PAY = 4 * MAIN + TILE
UP0 = 128
ROWS = TOK // 2


def permutation_matrix(shape, page_dim):
    col = lax.broadcasted_iota(jnp.int32, shape, page_dim)
    pos = lax.broadcasted_iota(jnp.int32, shape, 1 - page_dim)
    group = pos // 128
    lane = pos - group * 128
    inside = jnp.where(
        lane < MAIN,
        lane,
        jnp.where(lane < 2 * MAIN, lane + 2, jnp.where(lane < 98, lane - 48, lane)),
    )
    source = jnp.where(lane < 100, group * 100 + inside, -1)
    return jnp.where(col == source, 1.0, 0.0).astype(BF16)


def kernel(
    idx, masters, tokens_hbm, cot_hbm,
    out_masters, out_hidden, out_ig, out_grads,
    tok, cot, cotp, hid, outgoing, incoming, xs, xr, w, dbuf, dt, dwb, dwown,
    ra, rb, rc, fin, xs2, xr2, ig, igs, igr, zs, zr, ls, lr,
    psend, precv, ssem, rsem, lsem,
):
    dp = lax.axis_index("dp")
    me = lax.axis_index("shard")
    y, xh = dp // 2, dp % 2
    xl, z, core = me // 16, (me // 2) % 8, me % 2
    yr, yl, yo = (y + 1) % NY, (y + NY - 1) % NY, (y + 2) % NY
    right_y = (yr * 2 + xh, me)
    left_y = (yl * 2 + xh, me)
    xpartner = (y * 2 + 1 - xh, me)
    cpartner = (dp, me + 1 - 2 * core)
    lpartner = (dp, (1 - xl) * 16 + z * 2 + core)
    right_z = (dp, xl * 16 + ((z + 1) % NZ) * 2 + core)
    left_z = (dp, xl * 16 + ((z + NZ - 1) % NZ) * 2 + core)
    ydir = (right_y, left_y)
    zdir = (right_z, left_z)

    count = [0]

    def remote(src, dst, device):
        n = count[0]
        count[0] += 1
        return pltpu.make_async_remote_copy(
            src_ref=src, dst_ref=dst, send_sem=ssem.at[n], recv_sem=rsem.at[n],
            device_id=device, device_id_type=MESH,
        )

    started = []

    def start(copy):
        copy.start()
        started.append(copy)
        return copy

    load_tok = pltpu.make_async_copy(tokens_hbm, tok, lsem.at[0])
    load_cot = pltpu.make_async_copy(cot_hbm, cot, lsem.at[1])
    load_cot.start()
    load_tok.start()

    barrier = pltpu.get_barrier_semaphore()
    for peer in (right_y, left_y, xpartner):
        pl.semaphore_signal(barrier, inc=1, device_id=peer, device_id_type=MESH)

    def greet(k, carry):
        pl.semaphore_signal(
            barrier, inc=1, device_id=(dp, (me + k) % SHARDS), device_id_type=MESH
        )
        return carry

    lax.fori_loop(1, SHARDS, greet, 0)
    incoming[me] = jnp.zeros((1, 2 * D), F32)
    pl.semaphore_wait(barrier, 3 + SHARDS - 1)

    def page_copy(t):
        return pltpu.make_async_remote_copy(
            src_ref=outgoing.at[t], dst_ref=incoming.at[me],
            send_sem=psend.at[t], recv_sem=precv.at[me],
            device_id=(dp, t), device_id_type=MESH,
        )

    def page_out(k, carry):
        t = (me + k) % SHARDS
        outgoing[t] = masters[pl.ds(idx[t], 1), :]
        page_copy(t).start()
        return carry

    lax.fori_loop(1, SHARDS, page_out, 0)

    for g in range(NY):
        w[g, 112:128, :] = jnp.zeros((16, D), BF16)
        w[g, 240:256, :] = jnp.zeros((16, D), BF16)
    load_cot.wait()
    for r in range(4):
        rows = pl.ds(r * 256, 256)
        moved = jnp.dot(
            cot[rows, :], permutation_matrix((8 * PAGES, NY * 128), 0), preferred_element_type=F32
        ).astype(BF16)
        for g in range(NY):
            cotp[g, rows, :] = moved[:, g * 128 : (g + 1) * 128]
    load_tok.wait()

    def page_wait(k, carry):
        t = (me + k) % SHARDS
        pltpu.make_async_remote_copy(
            src_ref=outgoing.at[t], dst_ref=incoming.at[t],
            send_sem=psend.at[t], recv_sem=precv.at[t],
            device_id=(dp, t), device_id_type=MESH,
        ).wait()
        return carry

    lax.fori_loop(1, SHARDS, page_wait, 0)

    for j in range(PAGES):
        p = idx[SHARDS + j]
        out_masters[j : j + 1, :] = jnp.where(
            p < 0, masters[j : j + 1, :], incoming[jnp.maximum(p, 0)]
        )

    gate_at = pl.multiple_of(MAIN * xh, 16)
    gate_ot = pl.multiple_of(MAIN * (1 - xh), 16)
    up_at = pl.multiple_of(UP0 + MAIN * xh, 16)
    up_ot = pl.multiple_of(UP0 + MAIN * (1 - xh), 16)
    none = jnp.zeros((6, D), F32)
    xs[0:MAIN, :] = out_masters[0:MAIN, 0:D].astype(BF16)
    xs[MAIN : 2 * MAIN, :] = out_masters[0:MAIN, D:].astype(BF16)
    last = out_masters[MAIN:PAGES, :]
    xs[2 * MAIN :, :] = jnp.concatenate([last[:, 0:D], none, last[:, D:], none], axis=0).astype(BF16)
    xcopy = start(remote(xs, xr, xpartner))
    w[y, pl.ds(gate_at, MAIN), :] = xs[0:MAIN, :]
    w[y, pl.ds(up_at, MAIN), :] = xs[MAIN : 2 * MAIN, :]

    def wslice(g, at, size):
        return w.at[g, pl.ds(at, size), :]

    spans = ((gate_at, MAIN), (up_at, MAIN), (gate_ot, MAIN), (up_ot, MAIN), (96, TILE))
    direct = {}

    def send_span(p):
        for dirn in range(2):
            ref = wslice(y, *spans[p])
            direct[dirn, p] = start(remote(ref, ref, ydir[dirn]))

    send_span(0)
    send_span(1)
    xcopy.wait_recv()
    w[y, pl.ds(gate_ot, MAIN), :] = xr[0:MAIN, :]
    w[y, pl.ds(up_ot, MAIN), :] = xr[MAIN : 2 * MAIN, :]
    mine = xs[2 * MAIN :, :].astype(F32)
    theirs = xr[2 * MAIN :, :].astype(F32)
    first = jnp.where(xh == 0, mine, theirs)
    second = jnp.where(xh == 0, theirs, mine)
    none4 = jnp.zeros((4, D), F32)
    w[y, 96:112, :] = jnp.concatenate(
        [first[0:2], second[0:2], none4, first[8:10], second[8:10], none4], axis=0
    ).astype(BF16)
    send_span(2)
    send_span(3)
    send_span(4)

    def place_tile(g):
        t = w[g, 96:112, :].astype(F32)
        w[g, 224:240, :] = jnp.concatenate([t[8:16], t[0:8]], axis=0).astype(BF16)

    def forward_group(g, begin):
        @pl.loop(0, 2)
        def _(step):
            r = (step + 1 - xl) % 2
            rows = pl.ds(pl.multiple_of(r * ROWS, ROWS), ROWS)
            both = lax.dot_general(
                tok[rows, :], w[g], (((1,), (1,)), ((), ())), preferred_element_type=F32
            )
            gate, up = both[:, 0:128], both[:, 128:256]
            grad_in = cotp[g, rows, :].astype(F32)
            sig = jax.nn.sigmoid(gate)
            active = gate * sig
            hid[g, rows, :] = (active * up).astype(BF16)
            d_gate = (grad_in * up * sig * (1.0 + gate * (1.0 - sig))).astype(BF16)
            d_up = (grad_in * active).astype(BF16)
            dbuf[rows, 0:128] = d_gate
            dbuf[rows, 128:256] = d_up
            dt[0:128, rows] = d_gate.T
            dt[128:256, rows] = d_up.T
            at = pl.ds(pl.multiple_of(r * 8, 8), 8)
            for n in range(5):
                cols = pl.ds(n * 512, 512)
                term = jnp.dot(dbuf[rows, :], w[g, :, cols], preferred_element_type=F32)
                term = term.reshape(8, 2, 32, 512)
                if begin:
                    ig[at, :, :, cols] = term
                else:
                    ig[at, :, :, cols] = ig[at, :, :, cols] + term

    def page_grads(h):
        cols = pl.ds(h * HALF, HALF)
        return jnp.dot(dt[...], tok[:, cols], preferred_element_type=F32)

    def put_grads(dst, h, kind):
        cols = pl.ds(h * HALF, HALF)
        part = page_grads(h)
        dst[0:96, cols] = part[0:96].astype(kind)
        dst[96:112, cols] = jnp.concatenate([part[96:104], part[224:232]], axis=0).astype(kind)
        dst[112:208, cols] = part[128:224].astype(kind)

    place_tile(y)
    forward_group(y, True)
    put_grads(dwown, 0, F32)
    put_grads(dwown, 1, F32)

    onward = {}
    for p, dirn in ((0, 0), (1, 1), (2, 0), (3, 1), (4, 0)):
        direct[dirn, p].wait_recv()
        g = (yl, yr)[dirn]
        ref = wslice(g, *spans[p])
        onward[p] = start(remote(ref, ref, ydir[dirn]))

    early = []
    for dirn in (0, 1):
        for p in range(5):
            if (p, dirn) not in ((0, 0), (1, 1), (2, 0), (3, 1), (4, 0)):
                direct[dirn, p].wait_recv()
        g = (yl, yr)[dirn]
        slot = (1, 0)[dirn]
        place_tile(g)
        forward_group(g, False)
        put_grads(dwb.at[slot], 0, BF16)
        put_grads(dwb.at[slot], 1, BF16)
        to, h = (1, 0) if dirn == 0 else (0, 1)
        early.append((to, start(remote(dwb.at[slot, :, pl.ds(h * HALF, HALF)], ra.at[to], ydir[to]))))
    early = dict(early)

    for p in range(5):
        onward[p].wait_recv()
    place_tile(yo)
    forward_group(yo, False)

    corec = {}
    for k in range(2):
        c = (1 - xl, xl)[k]
        at = pl.ds(pl.multiple_of(c * 8, 8), 8)

        @pl.loop(0, 8)
        def _(i):
            igs[c * 8 + i] = ig[c * 8 + i, 1 - core].astype(BF16)

        corec[k] = start(remote(igs.at[at], igr.at[at], cpartner))

    far = {}
    for h in range(2):
        put_grads(dwb.at[2], h, BF16)
        for q in range(2):
            cols = pl.ds(h * HALF + q * QUART, QUART)
            far[h, q] = start(remote(dwb.at[2, :, cols], rb.at[h, q], ydir[h]))

    zc = {}

    def z_step(step, k):
        c = (1 - xl, xl)[k]
        if step == 1:
            corec[k].wait_recv()
        for dirn in range(2):
            owner = (z + (5 - step)) % NZ if dirn == 0 else (z + NZ - (5 - step)) % NZ
            at = c * 8 + owner
            if step == 1:
                cols = pl.ds(dirn * HALF, HALF)
                zs[dirn, 0, k, :, cols] = (
                    ig[at, core, :, cols] + igr[at, :, cols].astype(F32)
                ).astype(BF16)
                zc[1, k, dirn] = start(
                    remote(zs.at[dirn, 0, k, :, cols], zr.at[dirn, 0, k, :, cols], zdir[dirn])
                )
                continue
            zc[step - 1, k, dirn].wait_recv()
            for h in range(2):
                cols = pl.ds(h * HALF, HALF)
                term = ig[at, core, :, cols] + igr[at, :, cols].astype(F32)
                if step > 2 or h == dirn:
                    term = term + zr[dirn, step - 2, k, :, cols].astype(F32)
                zs[dirn, step - 1, k, :, cols] = term.astype(BF16)
            zc[step, k, dirn] = start(
                remote(zs.at[dirn, step - 1, k], zr.at[dirn, step - 1, k], zdir[dirn])
            )

    second_hop = {}

    def pass_on(q):
        for dirn in range(2):
            far[dirn, q].wait_recv()
            cols = pl.ds(dirn * HALF + q * QUART, QUART)
            dwb[dirn, :, cols] = (
                dwb[dirn, :, cols].astype(F32) + rb[dirn, q].astype(F32)
            ).astype(BF16)
            second_hop[dirn, q] = start(remote(dwb.at[dirn, :, cols], rc.at[dirn, q], ydir[dirn]))

    xc = {}

    def collect(q):
        for h in range(2):
            second_hop[h, q].wait_recv()
            if q == 0:
                early[1 - h].wait_recv()
            cols = pl.ds(h * HALF + q * QUART, QUART)
            here = pl.ds(q * QUART, QUART)

            def total(rows):
                return (
                    dwown[rows, cols]
                    + rc[h, q, rows, :].astype(F32)
                    + ra[1 - h, rows, here].astype(F32)
                )

            def rows_of(at, size):
                return pl.ds(pl.multiple_of(at, 16), size)

            xs2[h, q, 0:MAIN, :] = total(rows_of(MAIN * (1 - xh), MAIN)).astype(BF16)
            xs2[h, q, MAIN : 2 * MAIN, :] = total(rows_of(112 + MAIN * (1 - xh), MAIN)).astype(BF16)
            shared = total(pl.ds(96, TILE))
            xs2[h, q, 2 * MAIN :, :] = shared.astype(BF16)
            xc[h, q] = start(remote(xs2.at[h, q], xr2.at[h, q], xpartner))
            fin[0:MAIN, cols] = total(rows_of(MAIN * xh, MAIN))
            fin[MAIN : 2 * MAIN, cols] = total(rows_of(112 + MAIN * xh, MAIN))
            fin[2 * MAIN :, cols] = shared

    def finish(q):
        scale = 1.0 / math.sqrt(TOK * NY * NXH)
        for h in range(2):
            xc[h, q].wait_recv()
            cols = pl.ds(h * HALF + q * QUART, QUART)
            ucols = pl.ds(D + h * HALF + q * QUART, QUART)
            whole = (fin[:, cols] + xr2[h, q].astype(F32)) * scale
            out_grads[0:MAIN, cols] = whole[0:MAIN]
            out_grads[0:MAIN, ucols] = whole[MAIN : 2 * MAIN]
            t = whole[2 * MAIN :]
            out_grads[MAIN:PAGES, cols] = jnp.where(xh == 0, t[0:2], t[2:4])
            out_grads[MAIN:PAGES, ucols] = jnp.where(xh == 0, t[8:10], t[10:12])

    def z_total(k):
        c = (1 - xl, xl)[k]
        at = c * 8 + z
        for dirn in range(2):
            zc[4, k, dirn].wait_recv()
        return (
            ig[at, core]
            + igr[at].astype(F32)
            + zr[0, 3, k].astype(F32)
            + zr[1, 3, k].astype(F32)
        )

    z_step(1, 0)
    z_step(1, 1)
    z_step(2, 0)
    z_step(2, 1)
    for r in range(4):
        rows = pl.ds(r * 256, 256)
        flat = jnp.concatenate([hid[g, rows, :] for g in range(NY)], axis=1)
        out_hidden[rows, :] = jnp.dot(
            flat, permutation_matrix((NY * 128, 8 * PAGES), 1), preferred_element_type=F32
        ).astype(BF16)
    pass_on(0)
    z_step(3, 0)
    z_step(3, 1)
    pass_on(1)
    z_step(4, 0)
    z_step(4, 1)
    collect(0)
    ls[...] = z_total(0).astype(BF16)
    lcopy = start(remote(ls, lr, lpartner))
    collect(1)
    finish(0)
    own = z_total(1)
    lcopy.wait_recv()
    out_ig[...] = (own + lr[...].astype(F32)).astype(BF16)
    finish(1)
    for copy in started:
        copy.wait_send()


def body(tokens, masters, cotangent, partner, slots):
    member = lax.axis_index("shard")
    my_partner = lax.dynamic_index_in_dim(partner, member, 1, False)
    my_slot = lax.dynamic_index_in_dim(slots, member, 1, False)
    peers = jnp.arange(SHARDS, dtype=jnp.int32)
    pages = jnp.arange(PAGES, dtype=jnp.int32)
    give = jnp.sum(jnp.where(my_partner[:, None] == peers[None, :], my_slot[:, None], 0), axis=0)
    take = jnp.sum(jnp.where(my_slot[:, None] == pages[None, :], my_partner[:, None] + 1, 0), axis=0) - 1
    idx = jnp.concatenate([give, take])
    vmem = pl.BlockSpec(memory_space=pltpu.VMEM)
    n_remote = 64
    outs = pl.pallas_call(
        kernel,
        out_shape=(
            jax.ShapeDtypeStruct((PAGES, 2 * D), F32),
            jax.ShapeDtypeStruct((TOK, 8 * PAGES), BF16),
            jax.ShapeDtypeStruct((32, D), BF16),
            jax.ShapeDtypeStruct((PAGES, 2 * D), F32),
        ),
        in_specs=[
            pl.BlockSpec(memory_space=pltpu.SMEM),
            vmem,
            pl.BlockSpec(memory_space=pl.ANY),
            pl.BlockSpec(memory_space=pl.ANY),
        ],
        out_specs=(vmem,) * 4,
        scratch_shapes=[
            pltpu.VMEM((TOK, D), BF16),
            pltpu.VMEM((TOK, 8 * PAGES), BF16),
            pltpu.VMEM((NY, TOK, 128), BF16),
            pltpu.VMEM((NY, TOK, 128), BF16),
            pltpu.VMEM((SHARDS, 1, 2 * D), F32),
            pltpu.VMEM((SHARDS, 1, 2 * D), F32),
            pltpu.VMEM((112, D), BF16),
            pltpu.VMEM((112, D), BF16),
            pltpu.VMEM((NY, 256, D), BF16),
            pltpu.VMEM((TOK, 256), BF16),
            pltpu.VMEM((256, TOK), BF16),
            pltpu.VMEM((3, PAY, D), BF16),
            pltpu.VMEM((PAY, D), F32),
            pltpu.VMEM((2, PAY, HALF), BF16),
            pltpu.VMEM((2, 2, PAY, QUART), BF16),
            pltpu.VMEM((2, 2, PAY, QUART), BF16),
            pltpu.VMEM((112, D), F32),
            pltpu.VMEM((2, 2, 112, QUART), BF16),
            pltpu.VMEM((2, 2, 112, QUART), BF16),
            pltpu.VMEM((16, 2, 32, D), F32),
            pltpu.VMEM((16, 32, D), BF16),
            pltpu.VMEM((16, 32, D), BF16),
            pltpu.VMEM((2, 4, 2, 32, D), BF16),
            pltpu.VMEM((2, 4, 2, 32, D), BF16),
            pltpu.VMEM((32, D), BF16),
            pltpu.VMEM((32, D), BF16),
            pltpu.SemaphoreType.DMA((SHARDS,)),
            pltpu.SemaphoreType.DMA((SHARDS,)),
            pltpu.SemaphoreType.DMA((n_remote,)),
            pltpu.SemaphoreType.DMA((n_remote,)),
            pltpu.SemaphoreType.DMA((2,)),
        ],
        compiler_params=pltpu.CompilerParams(
            collective_id=0, has_side_effects=True, vmem_limit_bytes=60 * 2**20
        ),
    )(idx, masters[0], tokens, cotangent)
    new, hidden, input_grad, grads = outs
    return (new[None], hidden, input_grad, grads[None])


def solution(mesh):
    in_specs = (P("dp", None), P("dp", "shard", None), P("dp", "shard"), P(), P())
    out_specs = (
        P("dp", "shard", None),
        P("dp", "shard"),
        P(("dp", "shard"), None),
        P("dp", "shard", None),
    )
    return jax.shard_map(body, mesh=mesh, in_specs=in_specs, out_specs=out_specs, check_vma=False)
```

```python
import functools
import math

import jax
import jax.numpy as jnp
from jax import lax
from jax.experimental import pallas as pl
from jax.experimental.pallas import tpu as pltpu
from jax.sharding import PartitionSpec as P

MESH = pl.DeviceIdType.MESH
F32, BF16 = jnp.float32, jnp.bfloat16

NY, NXH, NXL, NZ, NC = 4, 2, 2, 8, 2
SHARDS = NXL * NZ * NC
MOVED = SHARDS - 1
PAGES = 50
KEPT = PAGES - MOVED
UNITS = NY * NXH * PAGES
D = 2560
TOK = 1024
HALF = D // 2
PIECES = 5
WIDE = HALF // PIECES
CROSS = 2
EARLY = 16
MAIN = 48
TILE = 16
PAY = 4 * MAIN + TILE
UP0 = 128
ROWS = TOK // 2
LANES = NY * 128
N_SENDS = 128


def prepare(partner, slots, idx, source):
    me = lax.axis_index("shard")

    def clear(j, carry):
        idx[SHARDS + j] = -1
        return carry

    lax.fori_loop(0, PAGES, clear, 0, unroll=True)

    def note(r, carry):
        p, s = partner[r, me], slots[r, me]
        idx[p] = s
        idx[SHARDS + s] = p
        return carry

    lax.fori_loop(0, MOVED, note, 0, unroll=True)
    lane = lax.broadcasted_iota(jnp.int32, (1, LANES), 1)
    group = lane // 128
    lane = lane - group * 128
    place = jnp.where(
        lane < 2 * MAIN, lane % MAIN, jnp.where(lane < 100, MAIN + lane % 2, -1)
    )
    block = jnp.where(lane < 2 * MAIN, lane // MAIN, (lane - 2 * MAIN) // 2)

    def put(j, carry):
        count, unit = carry
        p = idx[SHARDS + j]
        kept = p < 0
        at = jnp.where(kept, count, KEPT + (p + SHARDS - me - 1) % SHARDS)
        idx[SHARDS + PAGES + at] = j
        idx[SHARDS + 2 * PAGES + j] = at
        unit = jnp.where(place == at, j, unit)
        return count + jnp.where(kept, 1, 0), unit

    _, unit = lax.fori_loop(0, PAGES, put, (0, jnp.zeros((1, LANES), jnp.int32)), unroll=True)
    source[...] = jnp.where(place < 0, -1, group * (2 * PAGES) + block * PAGES + unit)


def kernel(
    idx, source, masters, tokens_hbm, cot_hbm,
    out_masters, out_hidden, out_ig, out_grads,
    tok, cot, cotp, hid, outgoing, incoming, stage, tx, tr, w, wo, d, do, dt, dwb, dwown,
    ra, rx, sb, rb, rc, fin, xs2, xr2, ig, zs, zr, ls, lr,
    psend, precv, ssem, rsem, lsem,
):
    dp = lax.axis_index("dp")
    me = lax.axis_index("shard")
    y, xh = dp // 2, dp % 2
    xl, z, core = me // 16, (me // 2) % 8, me % 2
    yr, yl, yo = (y + 1) % NY, (y + NY - 1) % NY, (y + 2) % NY
    right_y = (yr * 2 + xh, me)
    left_y = (yl * 2 + xh, me)
    xpartner = (y * 2 + 1 - xh, me)
    cpartner = (dp, me + 1 - 2 * core)
    lpartner = (dp, (1 - xl) * 16 + z * 2 + core)
    right_z = (dp, xl * 16 + ((z + 1) % NZ) * 2 + core)
    left_z = (dp, xl * 16 + ((z + NZ - 1) % NZ) * 2 + core)
    ydir = (right_y, left_y)
    zdir = (right_z, left_z)

    count = [0]
    started = []

    def send(src, dst, device):
        n = count[0]
        count[0] += 1
        copy = pltpu.make_async_remote_copy(
            src_ref=src, dst_ref=dst, send_sem=ssem.at[n], recv_sem=rsem.at[n],
            device_id=device, device_id_type=MESH,
        )
        copy.start()
        started.append(copy)
        return copy

    load_tok = pltpu.make_async_copy(tokens_hbm, tok, lsem.at[0])
    load_cot = pltpu.make_async_copy(cot_hbm, cot, lsem.at[1])
    load_cot.start()
    load_tok.start()

    barrier = pltpu.get_barrier_semaphore()
    for peer in (right_y, left_y, xpartner):
        pl.semaphore_signal(barrier, inc=1, device_id=peer, device_id_type=MESH)

    def greet(k, carry):
        pl.semaphore_signal(
            barrier, inc=1, device_id=(dp, (me + k) % SHARDS), device_id_type=MESH
        )
        return carry

    lax.fori_loop(1, SHARDS, greet, 0)
    incoming[me] = jnp.zeros((1, 2 * D), F32)

    def page_fill(k, carry):
        t = (me + k) % SHARDS
        outgoing[t] = masters[idx[t]]
        return carry

    lax.fori_loop(1, SHARDS, page_fill, 0)

    def at(kind, b, part):
        return pl.multiple_of(kind * UP0 + MAIN * b + (0, EARLY)[part], 16)

    size = (EARLY, MAIN - EARLY)

    def span(g, kind, b, part):
        return w.at[g, pl.ds(at(kind, b, part), size[part]), :]

    def put_block(part):
        begin = (0, EARLY)[part]
        for kind in range(2):
            w[y, pl.ds(at(kind, xh, part), size[part]), :] = stage[
                begin : begin + size[part], kind * D : (kind + 1) * D
            ].astype(BF16)

    for i in range(EARLY):
        stage[i : i + 1, :] = masters[idx[SHARDS + PAGES + i]]
    put_block(0)

    pl.semaphore_wait(barrier, 3 + SHARDS - 1)

    def page_out(k, carry):
        t = (me + k) % SHARDS
        pltpu.make_async_remote_copy(
            src_ref=outgoing.at[t], dst_ref=incoming.at[me],
            send_sem=psend.at[t], recv_sem=precv.at[me],
            device_id=(dp, t), device_id_type=MESH,
        ).start()
        return carry

    other = 1 - xh
    xa, own, ot, fwd, x2 = {}, {}, {}, {}, {}

    def spread(table, kind, b, part):
        for dirn in range(2):
            ref = span(y, kind, b, part)
            table[kind, part, dirn] = send(ref, ref, ydir[dirn])

    def give_x(part):
        for kind in range(2):
            ref = span(y, kind, xh, part)
            xa[kind, part] = send(ref, ref, xpartner)

    def take_x(part):
        for kind in range(2):
            xa[kind, part].wait_recv()
            spread(ot, kind, other, part)

    def forward_on(part):
        for kind in range(2):
            own[kind, part, kind].wait_recv()
            ref = span((yl, yr)[kind], kind, xh, part)
            fwd[kind, part] = send(ref, ref, ydir[kind])

    def cross(part):
        for kind in range(2):
            fwd[kind, part].wait_recv()
            ref = span(yo, kind, xh, part)
            x2[kind, part] = send(ref, ref, xpartner)

    lax.fori_loop(1, SHARDS, page_out, 0)
    give_x(0)
    for kind in range(2):
        spread(own, kind, xh, 0)
    for g in range(NY):
        for ref in (w, wo):
            ref[g, 112:128, :] = jnp.zeros((16, D), BF16)
            ref[g, 240:256, :] = jnp.zeros((16, D), BF16)

    def matrix():
        unit = lax.broadcasted_iota(jnp.int32, (UNITS, LANES), 0)
        return jnp.where(unit == source[...], 1.0, 0.0).astype(BF16)

    take_x(0)
    load_cot.wait()
    for r in range(2):
        rows = pl.ds(r * ROWS, ROWS)
        moved = lax.dot_general(
            cot[:, rows], matrix(), (((0,), (0,)), ((), ())), preferred_element_type=F32
        ).astype(BF16)
        for g in range(NY):
            cotp[g, rows, :] = moved[:, g * 128 : (g + 1) * 128]
    forward_on(0)
    load_tok.wait()
    cross(0)

    for i in range(EARLY, KEPT):
        stage[i : i + 1, :] = masters[idx[SHARDS + PAGES + i]]

    def page_wait(k, carry):
        t = (me + k) % SHARDS
        pltpu.make_async_remote_copy(
            src_ref=outgoing.at[t], dst_ref=incoming.at[t],
            send_sem=psend.at[t], recv_sem=precv.at[t],
            device_id=(dp, t), device_id_type=MESH,
        ).wait()
        return carry

    lax.fori_loop(1, SHARDS, page_wait, 0)
    for k in range(MOVED):
        stage[KEPT + k : KEPT + k + 1, :] = incoming[(me + 1 + k) % SHARDS]
    put_block(1)
    give_x(1)
    none = jnp.zeros((6, D), F32)
    last = stage[MAIN:PAGES, :]
    tx[...] = jnp.concatenate([last[:, 0:D], none, last[:, D:], none], axis=0).astype(BF16)
    tcopy = send(tx, tr, xpartner)
    for kind in range(2):
        spread(own, kind, xh, 1)

    for j in range(PAGES):
        p = idx[SHARDS + j]
        out_masters[j] = jnp.where(p < 0, masters[j], incoming[jnp.maximum(p, 0)])

    forward_on(1)
    take_x(1)
    tcopy.wait_recv()
    mine, theirs = tx[...].astype(F32), tr[...].astype(F32)
    first = jnp.where(xh == 0, mine, theirs)
    second = jnp.where(xh == 0, theirs, mine)
    none4 = jnp.zeros((4, D), F32)
    w[y, 96:112, :] = jnp.concatenate(
        [first[0:2], second[0:2], none4, first[8:10], second[8:10], none4], axis=0
    ).astype(BF16)
    shared = {}
    for dirn in range(2):
        ref = w.at[y, 96:112, :]
        shared[dirn] = send(ref, ref, ydir[dirn])

    def place_tile(ref):
        t = ref[96:112, :].astype(F32)
        ref[224:240, :] = jnp.concatenate([t[8:16], t[0:8]], axis=0).astype(BF16)

    cw, cd = {}, {}

    def share_group(name, g):
        place_tile(w.at[g])
        cw[name] = [
            send(w.at[g, rows, :], wo.at[g, rows, :], cpartner)
            for rows in (pl.ds(0, 112), pl.ds(UP0, 96))
        ]

    def forward_group(name, g):
        @pl.loop(0, 2)
        def _(r):
            rows = pl.ds(pl.multiple_of(r * ROWS, ROWS), ROWS)
            both = lax.dot_general(
                tok[rows, :], w[g], (((1,), (1,)), ((), ())), preferred_element_type=F32
            )
            gate, up = both[:, 0:128], both[:, 128:256]
            grad_in = cotp[g, rows, :].astype(F32)
            sig = jax.nn.sigmoid(gate)
            active = gate * sig
            hid[rows, pl.ds(pl.multiple_of(g * 128, 128), 128)] = (active * up).astype(BF16)
            d_gate = (grad_in * up * sig * (1.0 + gate * (1.0 - sig))).astype(BF16)
            d_up = (grad_in * active).astype(BF16)
            half = pl.ds(pl.multiple_of(r * 8, 8), 8)
            for k, part in ((0, d_gate), (1, d_up)):
                part4 = part.reshape(8, 2, 32, 128)
                for c in range(2):
                    d[g, c, half, :, k * 128 : (k + 1) * 128] = part4[:, c]
                dt[name, k * 128 : (k + 1) * 128, rows] = part.T

        cd[name] = send(d.at[g, 1 - core], do.at[g], cpartner)

    def token_terms(groups, begin):
        @pl.loop(0, 2)
        def _(step):
            r = (step + 1 - xl) % 2
            half = pl.ds(pl.multiple_of(r * 8, 8), 8)
            for n in range(5):
                cols = pl.ds(n * 512, 512)
                terms = [] if begin else [ig[half, :, cols].reshape(256, 512)]
                for g in groups:
                    for left, right in ((d.at[g, core], w.at[g]), (do.at[g], wo.at[g])):
                        terms.append(
                            jnp.dot(
                                left[half].reshape(256, 256), right[:, cols],
                                preferred_element_type=F32,
                            )
                        )
                ig[half, :, cols] = functools.reduce(jnp.add, terms).reshape(8, 32, 512)

    def put_grads(name, dst, h, kind):
        cols = pl.ds(h * HALF, HALF)
        part = jnp.dot(dt[name], tok[:, cols], preferred_element_type=F32)
        dst[0:96, cols] = part[0:96].astype(kind)
        dst[96:112, cols] = jnp.concatenate([part[96:104], part[224:232]], axis=0).astype(kind)
        dst[112:208, cols] = part[128:224].astype(kind)

    def core_wait(name, g):
        for copy in cw[name]:
            copy.wait_recv()
        place_tile(wo.at[g])
        cd[name].wait_recv()

    RIGHT, LEFT, FAR, OWN = range(4)
    share_group(OWN, y)
    forward_group(OWN, y)
    cross(1)
    shared[0].wait_recv()
    ref = w.at[yl, 96:112, :]
    onward = send(ref, ref, right_y)
    put_grads(OWN, dwown, 0, F32)
    put_grads(OWN, dwown, 1, F32)
    core_wait(OWN, y)
    token_terms((y,), True)

    early = {}
    for dirn, name, g in ((0, LEFT, yl), (1, RIGHT, yr)):
        for kind in range(2):
            for part in range(2):
                ot[kind, part, dirn].wait_recv()
                if kind != dirn:
                    own[kind, part, dirn].wait_recv()
        if dirn == 1:
            shared[1].wait_recv()
        share_group(name, g)
        forward_group(name, g)
        to, h = (1, 0) if dirn == 0 else (0, 1)
        put_grads(name, dwb.at[name], h, BF16)
        early[to] = send(dwb.at[name, :, pl.ds(h * HALF, HALF)], ra.at[to], ydir[to])

    for kind in range(2):
        for part in range(2):
            x2[kind, part].wait_recv()
    onward.wait_recv()
    share_group(FAR, yo)
    forward_group(FAR, yo)
    core_wait(LEFT, yl)
    core_wait(RIGHT, yr)
    core_wait(FAR, yo)
    token_terms((yl, yr, yo), False)

    zc = {}

    def z_step(step, k):
        c = (1 - xl, xl)[k]
        for dirn in range(2):
            owner = (z + (5 - step)) % NZ if dirn == 0 else (z + NZ - (5 - step)) % NZ
            row = c * 8 + owner
            if step == 1:
                cols = pl.ds(dirn * HALF, HALF)
                zs[dirn, 0, k, :, cols] = ig[row, :, cols].astype(BF16)
                zc[1, k, dirn] = send(
                    zs.at[dirn, 0, k, :, cols], zr.at[dirn, 0, k, :, cols], zdir[dirn]
                )
                continue
            zc[step - 1, k, dirn].wait_recv()
            for h in range(2):
                cols = pl.ds(h * HALF, HALF)
                term = ig[row, :, cols]
                if step > 2 or h == dirn:
                    term = term + zr[dirn, step - 2, k, :, cols].astype(F32)
                zs[dirn, step - 1, k, :, cols] = term.astype(BF16)
            zc[step, k, dirn] = send(zs.at[dirn, step - 1, k], zr.at[dirn, step - 1, k], zdir[dirn])

    z_step(1, 0)
    z_step(1, 1)

    gate_own = pl.ds(pl.multiple_of(MAIN * xh, 16), MAIN)
    gate_ot = pl.ds(pl.multiple_of(MAIN * other, 16), MAIN)
    up_own = pl.ds(pl.multiple_of(112 + MAIN * xh, 16), MAIN)
    up_ot = pl.ds(pl.multiple_of(112 + MAIN * other, 16), MAIN)
    tile = pl.ds(96, TILE)

    def columns(h, q):
        return pl.ds(h * HALF + q * WIDE, WIDE)

    across, far, second_hop, xc = {}, {}, {}, {}
    for h in range(2):
        put_grads(FAR, dwb.at[FAR], h, BF16)
        for q in range(CROSS):
            across[h, q] = [
                send(dwb.at[FAR, gate_ot, columns(h, q)], rx.at[h, q, 0:MAIN, :], xpartner),
                send(dwb.at[FAR, up_ot, columns(h, q)], rx.at[h, q, MAIN : 2 * MAIN, :], xpartner),
            ]
        for q in range(CROSS, PIECES):
            far[h, q] = send(dwb.at[FAR, :, columns(h, q)], rb.at[h, q], ydir[h])
    put_grads(LEFT, dwb.at[LEFT], 1, BF16)
    put_grads(RIGHT, dwb.at[RIGHT], 0, BF16)

    def join(q):
        for h in range(2):
            for copy in across[h, q]:
                copy.wait_recv()
            cols = columns(h, q)
            for rows, begin in ((gate_own, 0), (up_own, MAIN)):
                sb[h, q, begin : begin + MAIN, :] = (
                    dwb[FAR, rows, cols].astype(F32) + rx[h, q, begin : begin + MAIN, :].astype(F32)
                ).astype(BF16)
            sb[h, q, 2 * MAIN :, :] = dwb[FAR, tile, cols]
            far[h, q] = send(sb.at[h, q], rb.at[h, q, 0:112, :], ydir[h])

    def pass_on(q):
        for h in range(2):
            far[h, q].wait_recv()
            cols = columns(h, q)
            if q < CROSS:
                parts = ((gate_own, 0, MAIN), (up_own, MAIN, MAIN), (tile, 2 * MAIN, TILE))
            else:
                parts = ((pl.ds(0, PAY), 0, PAY),)
            for rows, begin, n in parts:
                dwb[h, rows, cols] = (
                    dwb[h, rows, cols].astype(F32) + rb[h, q, begin : begin + n, :].astype(F32)
                ).astype(BF16)
            second_hop[h, q] = send(dwb.at[h, :, cols], rc.at[h, q], ydir[h])

    def collect(q):
        for h in range(2):
            second_hop[h, q].wait_recv()
            if q == CROSS:
                early[1 - h].wait_recv()
            cols = columns(h, q)
            here = pl.ds(q * WIDE, WIDE)

            def total(rows):
                return (
                    dwown[rows, cols]
                    + rc[h, q, rows, :].astype(F32)
                    + ra[1 - h, rows, here].astype(F32)
                )

            xs2[h, q, 0:MAIN, :] = total(gate_ot).astype(BF16)
            xs2[h, q, MAIN : 2 * MAIN, :] = total(up_ot).astype(BF16)
            both = total(tile)
            xs2[h, q, 2 * MAIN :, :] = both.astype(BF16)
            xc[h, q] = send(xs2.at[h, q], xr2.at[h, q], xpartner)
            fin[0:MAIN, cols] = total(gate_own)
            fin[MAIN : 2 * MAIN, cols] = total(up_own)
            fin[2 * MAIN :, cols] = both

    def finish(q):
        scale = 1.0 / math.sqrt(TOK * NY * NXH)
        for h in range(2):
            xc[h, q].wait_recv()
            cols = columns(h, q)
            ucols = pl.ds(D + h * HALF + q * WIDE, WIDE)
            fin[:, cols] = (fin[:, cols] + xr2[h, q].astype(F32)) * scale
            for j in range(PAGES):
                p = idx[SHARDS + 2 * PAGES + j]
                rest = 2 * MAIN + 2 * xh + p - MAIN
                row = jnp.where(p < MAIN, p, rest)
                urow = jnp.where(p < MAIN, MAIN + p, rest + 8)
                out_grads[j, :, cols] = fin[pl.ds(row, 1), cols]
                out_grads[j, :, ucols] = fin[pl.ds(urow, 1), cols]

    def z_total(k):
        row = (1 - xl, xl)[k] * 8 + z
        for dirn in range(2):
            zc[4, k, dirn].wait_recv()
        return ig[row] + zr[0, 3, k].astype(F32) + zr[1, 3, k].astype(F32)

    z_step(2, 0)
    join(0)
    pass_on(2)
    z_step(2, 1)
    join(1)
    pass_on(3)
    z_step(3, 0)
    pass_on(4)
    pass_on(0)
    z_step(3, 1)
    pass_on(1)
    collect(2)
    z_step(4, 0)
    collect(3)
    z_step(4, 1)
    for r in range(2):
        rows = pl.ds(r * ROWS, ROWS)
        out_hidden[:, rows] = lax.dot_general(
            matrix(), hid[rows, :], (((1,), (1,)), ((), ())), preferred_element_type=F32
        ).astype(BF16)
    collect(4)
    ls[...] = z_total(0).astype(BF16)
    lcopy = send(ls, lr, lpartner)
    collect(0)
    finish(2)
    collect(1)
    finish(3)
    finish(4)
    own_sum = z_total(1)
    lcopy.wait_recv()
    out_ig[...] = (own_sum + lr[...].astype(F32)).astype(BF16)
    finish(0)
    finish(1)

    for copy in started:
        copy.wait_send()


def hand_over(*refs):
    ins, outs, held, (arrive, leave) = refs[0:4], refs[4:8], refs[8:12], refs[12:14]
    reads = [pltpu.make_async_copy(ins[i], held[i], arrive.at[i]) for i in range(4)]
    writes = [pltpu.make_async_copy(held[i], outs[i], leave.at[i]) for i in range(4)]
    for copy in reads:
        copy.start()
    for read, write in zip(reads, writes):
        read.wait()
        write.start()
    for copy in writes:
        copy.wait()


def body(tokens, masters, cotangent, partner, slots):
    vmem = pl.BlockSpec(memory_space=pltpu.VMEM)
    smem = pl.BlockSpec(memory_space=pltpu.SMEM)
    idx, source = pl.pallas_call(
        prepare,
        out_shape=(
            jax.ShapeDtypeStruct((SHARDS + 3 * PAGES,), jnp.int32),
            jax.ShapeDtypeStruct((1, LANES), jnp.int32),
        ),
        in_specs=[smem, smem],
        out_specs=(smem, vmem),
    )(partner, slots)
    outs = pl.pallas_call(
        kernel,
        out_shape=(
            jax.ShapeDtypeStruct((PAGES, 1, 2 * D), F32),
            jax.ShapeDtypeStruct((UNITS, TOK), BF16),
            jax.ShapeDtypeStruct((32, D), BF16),
            jax.ShapeDtypeStruct((PAGES, 1, 2 * D), F32),
        ),
        in_specs=[
            smem,
            vmem,
            vmem,
            pl.BlockSpec(memory_space=pl.ANY),
            pl.BlockSpec(memory_space=pl.ANY),
        ],
        out_specs=(vmem,) * 4,
        scratch_shapes=[
            pltpu.VMEM((TOK, D), BF16),
            pltpu.VMEM((UNITS, TOK), BF16),
            pltpu.VMEM((NY, TOK, 128), BF16),
            pltpu.VMEM((TOK, LANES), BF16),
            pltpu.VMEM((SHARDS, 1, 2 * D), F32),
            pltpu.VMEM((SHARDS, 1, 2 * D), F32),
            pltpu.VMEM((PAGES + 6, 2 * D), F32),
            pltpu.VMEM((TILE, D), BF16),
            pltpu.VMEM((TILE, D), BF16),
            pltpu.VMEM((NY, 256, D), BF16),
            pltpu.VMEM((NY, 256, D), BF16),
            pltpu.VMEM((NY, 2, 16, 32, 256), BF16),
            pltpu.VMEM((NY, 16, 32, 256), BF16),
            pltpu.VMEM((4, 256, TOK), BF16),
            pltpu.VMEM((3, PAY, D), BF16),
            pltpu.VMEM((PAY, D), F32),
            pltpu.VMEM((2, PAY, HALF), BF16),
            pltpu.VMEM((2, CROSS, 2 * MAIN, WIDE), BF16),
            pltpu.VMEM((2, CROSS, 112, WIDE), BF16),
            pltpu.VMEM((2, PIECES, PAY, WIDE), BF16),
            pltpu.VMEM((2, PIECES, PAY, WIDE), BF16),
            pltpu.VMEM((112, D), F32),
            pltpu.VMEM((2, PIECES, 112, WIDE), BF16),
            pltpu.VMEM((2, PIECES, 112, WIDE), BF16),
            pltpu.VMEM((16, 32, D), F32),
            pltpu.VMEM((2, 4, 2, 32, D), BF16),
            pltpu.VMEM((2, 4, 2, 32, D), BF16),
            pltpu.VMEM((32, D), BF16),
            pltpu.VMEM((32, D), BF16),
            pltpu.SemaphoreType.DMA((SHARDS,)),
            pltpu.SemaphoreType.DMA((SHARDS,)),
            pltpu.SemaphoreType.DMA((N_SENDS,)),
            pltpu.SemaphoreType.DMA((N_SENDS,)),
            pltpu.SemaphoreType.DMA((2,)),
        ],
        compiler_params=pltpu.CompilerParams(
            collective_id=0, has_side_effects=True, vmem_limit_bytes=60 * 2**20
        ),
    )(idx, source, jnp.transpose(masters, (1, 0, 2)), tokens, cotangent.T)
    new, hidden, input_grad, grads = pl.pallas_call(
        hand_over,
        out_shape=tuple(jax.ShapeDtypeStruct(out.shape, out.dtype) for out in outs),
        in_specs=[pl.BlockSpec(memory_space=pl.ANY)] * 4,
        out_specs=(pl.BlockSpec(memory_space=pl.ANY),) * 4,
        scratch_shapes=[pltpu.VMEM(out.shape, out.dtype) for out in outs]
        + [pltpu.SemaphoreType.DMA((4,))] * 2,
    )(*outs)
    return (
        jnp.transpose(new, (1, 0, 2)),
        hidden.T,
        input_grad,
        jnp.transpose(grads, (1, 0, 2)),
    )


def solution(mesh):
    in_specs = (P("dp", None), P("dp", "shard", None), P("dp", "shard"), P(), P())
    out_specs = (
        P("dp", "shard", None),
        P("dp", "shard"),
        P(("dp", "shard"), None),
        P("dp", "shard", None),
    )
    return jax.shard_map(body, mesh=mesh, in_specs=in_specs, out_specs=out_specs, check_vma=False)
```

```python
import functools
import math

import jax
import jax.numpy as jnp
from jax import lax
from jax.experimental import pallas as pl
from jax.experimental.pallas import tpu as pltpu
from jax.sharding import PartitionSpec as P

MESH = pl.DeviceIdType.MESH
F32, BF16 = jnp.float32, jnp.bfloat16

NY, NXH, NXL, NZ, NC = 4, 2, 2, 8, 2
SHARDS = NXL * NZ * NC
MOVED = SHARDS - 1
PAGES = 50
KEPT = PAGES - MOVED
UNITS = NY * NXH * PAGES
D = 2560
TOK = 1024
HALF = D // 2
PIECES = 5
WIDE = HALF // PIECES
CROSS = 2
PART = 16
FIRST = 2 * PART - KEPT
MAIN = 48
TILE = 16
PAY = 4 * MAIN + TILE
UP0 = 128
ROWS = TOK // 2
LANES = NY * 128
N_SENDS = 128


def total(mask, value, axis):
    return jnp.sum(jnp.where(mask, value, 0), axis=axis, keepdims=True)


def plan(me, partner, slots, table, source):
    def iota(shape, axis):
        return lax.broadcasted_iota(jnp.int32, shape, axis)

    mine = iota((MOVED, SHARDS), 1) == me
    peer_c, slot_c = total(mine, partner[...], 1), total(mine, slots[...], 1)
    sub, lane = iota((MOVED, 128), 0), iota((MOVED, 128), 1)
    peer_r, slot_r = total(sub == lane, peer_c, 0), total(sub == lane, slot_c, 0)
    give_r = total(lane == peer_c, slot_c, 0)
    take_r = total(lane == slot_c, peer_c + 1, 0) - 1
    sub, lane = iota((64, 128), 0), iota((64, 128), 1)
    take_c = total((sub == slot_r) & (lane < MOVED), peer_r + 1, 1) - 1

    def place(take, before):
        ahead = take - me - 1
        return jnp.where(take < 0, before, KEPT + jnp.where(ahead < 0, ahead + SHARDS, ahead))

    place_r = place(take_r, total((take_c < 0) & (sub < PAGES) & (sub < lane), 1, 0))
    place_c = place(take_c, total((take_r < 0) & (lane < PAGES) & (lane < sub), 1, 1))
    order_r = total((place_c == lane) & (sub < PAGES), sub, 0)
    for i, row in enumerate((give_r, take_r, order_r, place_r)):
        table[i : i + 1, :] = row
    lane = iota((1, LANES), 1)
    group = lane // 128
    lane = lane - group * 128
    at = jnp.where(lane < 2 * MAIN, lane % MAIN, jnp.where(lane < 100, MAIN + lane % 2, -1))
    block = jnp.where(lane < 2 * MAIN, lane // MAIN, (lane - 2 * MAIN) // 2)
    sub = iota((64, LANES), 0)
    unit = total((place_c == at) & (sub < PAGES), sub, 0)
    source[...] = jnp.where(at < 0, -1, group * (2 * PAGES) + block * PAGES + unit)


def kernel(
    partner, slots, masters, tokens_hbm, cot_hbm,
    out_masters, out_hidden, out_ig, out_grads,
    table, idx, source, tok, cot, cotp, hid, outgoing, incoming, stage, tx, tr, w, wo, d, do, dt, dwb, dwown,
    ra, rx, sb, rb, rc, fin, xs2, xr2, ig, zs, zr, ls, lr,
    psend, precv, ssem, rsem, lsem,
):
    dp = lax.axis_index("dp")
    me = lax.axis_index("shard")
    y, xh = dp // 2, dp % 2
    xl, z, core = me // 16, (me // 2) % 8, me % 2
    yr, yl, yo = (y + 1) % NY, (y + NY - 1) % NY, (y + 2) % NY
    right_y = (yr * 2 + xh, me)
    left_y = (yl * 2 + xh, me)
    xpartner = (y * 2 + 1 - xh, me)
    cpartner = (dp, me + 1 - 2 * core)
    lpartner = (dp, (1 - xl) * 16 + z * 2 + core)
    right_z = (dp, xl * 16 + ((z + 1) % NZ) * 2 + core)
    left_z = (dp, xl * 16 + ((z + NZ - 1) % NZ) * 2 + core)
    ydir = (right_y, left_y)
    zdir = (right_z, left_z)

    count = [0]
    started = []

    def send(src, dst, device):
        n = count[0]
        count[0] += 1
        copy = pltpu.make_async_remote_copy(
            src_ref=src, dst_ref=dst, send_sem=ssem.at[n], recv_sem=rsem.at[n],
            device_id=device, device_id_type=MESH,
        )
        copy.start()
        started.append(copy)
        return copy

    load_tok = pltpu.make_async_copy(tokens_hbm, tok, lsem.at[0])
    load_cot = pltpu.make_async_copy(cot_hbm, cot, lsem.at[1])
    load_cot.start()
    load_tok.start()

    barrier = pltpu.get_barrier_semaphore()
    for peer in (right_y, left_y, xpartner):
        pl.semaphore_signal(barrier, inc=1, device_id=peer, device_id_type=MESH)

    def greet(k, carry):
        pl.semaphore_signal(
            barrier, inc=1, device_id=(dp, (me + k) % SHARDS), device_id_type=MESH
        )
        return carry

    lax.fori_loop(1, SHARDS, greet, 0)
    plan(me, partner, slots, table, source)
    load_idx = pltpu.make_async_copy(table, idx, lsem.at[2])
    load_idx.start()
    incoming[me] = jnp.zeros((1, 2 * D), F32)
    load_idx.wait()

    def page_fill(k, carry):
        t = (me + k) % SHARDS
        outgoing[t] = masters[idx[0, t]]
        return carry

    lax.fori_loop(1, SHARDS, page_fill, 0)

    def at(kind, b, part):
        return pl.multiple_of(kind * UP0 + MAIN * b + PART * part, 16)

    def span(g, kind, b, part):
        return w.at[g, pl.ds(at(kind, b, part), PART), :]

    def put_block(part):
        begin = PART * part
        for kind in range(2):
            w[y, pl.ds(at(kind, xh, part), PART), :] = stage[
                begin : begin + PART, kind * D : (kind + 1) * D
            ].astype(BF16)

    for i in range(PART):
        stage[i : i + 1, :] = masters[idx[2, i]]

    pl.semaphore_wait(barrier, 3 + SHARDS - 1)

    def page_out(k, carry):
        t = (me + k) % SHARDS
        pltpu.make_async_remote_copy(
            src_ref=outgoing.at[t], dst_ref=incoming.at[me],
            send_sem=psend.at[t], recv_sem=precv.at[me],
            device_id=(dp, t), device_id_type=MESH,
        ).start()
        return carry

    other = 1 - xh
    xa, own, ot, fwd, x2 = {}, {}, {}, {}, {}

    def spread(table, kind, b, part):
        for dirn in range(2):
            ref = span(y, kind, b, part)
            table[kind, part, dirn] = send(ref, ref, ydir[dirn])

    def give_x(part):
        for kind in range(2):
            ref = span(y, kind, xh, part)
            xa[kind, part] = send(ref, ref, xpartner)

    def take_x(part):
        for kind in range(2):
            xa[kind, part].wait_recv()
            spread(ot, kind, other, part)

    def forward_on(part):
        for kind in range(2):
            own[kind, part, kind].wait_recv()
            ref = span((yl, yr)[kind], kind, xh, part)
            fwd[kind, part] = send(ref, ref, ydir[kind])

    def cross(part):
        for kind in range(2):
            fwd[kind, part].wait_recv()
            ref = span(yo, kind, xh, part)
            x2[kind, part] = send(ref, ref, xpartner)

    def own_out(part):
        put_block(part)
        give_x(part)
        for kind in range(2):
            spread(own, kind, xh, part)

    lax.fori_loop(1, FIRST + 1, page_out, 0)
    own_out(0)
    lax.fori_loop(FIRST + 1, SHARDS, page_out, 0)
    for g in range(NY):
        for ref in (w, wo):
            ref[g, 112:128, :] = jnp.zeros((16, D), BF16)
            ref[g, 240:256, :] = jnp.zeros((16, D), BF16)

    def matrix():
        unit = lax.broadcasted_iota(jnp.int32, (UNITS, LANES), 0)
        return jnp.where(unit == source[...], 1.0, 0.0).astype(BF16)

    def page_wait(k, carry):
        t = (me + k) % SHARDS
        pltpu.make_async_remote_copy(
            src_ref=outgoing.at[t], dst_ref=incoming.at[t],
            send_sem=psend.at[t], recv_sem=precv.at[t],
            device_id=(dp, t), device_id_type=MESH,
        ).wait()
        return carry

    def pages_in(begin, end):
        lax.fori_loop(begin + 1, end + 1, page_wait, 0)
        for k in range(begin, end):
            stage[KEPT + k : KEPT + k + 1, :] = incoming[(me + 1 + k) % SHARDS]

    for i in range(PART, KEPT):
        stage[i : i + 1, :] = masters[idx[2, i]]
    take_x(0)
    forward_on(0)
    load_cot.wait()
    for r in range(2):
        rows = pl.ds(r * ROWS, ROWS)
        moved = lax.dot_general(
            cot[:, rows], matrix(), (((0,), (0,)), ((), ())), preferred_element_type=F32
        ).astype(BF16)
        for g in range(NY):
            cotp[g, rows, :] = moved[:, g * 128 : (g + 1) * 128]
    load_tok.wait()
    pages_in(0, FIRST)
    own_out(1)
    take_x(1)
    forward_on(1)
    pages_in(FIRST, MOVED)
    own_out(2)
    none = jnp.zeros((6, D), F32)
    last = stage[MAIN:PAGES, :]
    tx[...] = jnp.concatenate([last[:, 0:D], none, last[:, D:], none], axis=0).astype(BF16)
    tcopy = send(tx, tr, xpartner)
    cross(0)
    cross(1)

    for j in range(PAGES):
        p = idx[1, j]
        out_masters[j] = jnp.where(p < 0, masters[j], incoming[jnp.maximum(p, 0)])

    take_x(2)
    forward_on(2)
    tcopy.wait_recv()
    mine, theirs = tx[...].astype(F32), tr[...].astype(F32)
    first = jnp.where(xh == 0, mine, theirs)
    second = jnp.where(xh == 0, theirs, mine)
    none4 = jnp.zeros((4, D), F32)
    w[y, 96:112, :] = jnp.concatenate(
        [first[0:2], second[0:2], none4, first[8:10], second[8:10], none4], axis=0
    ).astype(BF16)
    shared = {}
    for dirn in range(2):
        ref = w.at[y, 96:112, :]
        shared[dirn] = send(ref, ref, ydir[dirn])

    def place_tile(ref):
        t = ref[96:112, :].astype(F32)
        ref[224:240, :] = jnp.concatenate([t[8:16], t[0:8]], axis=0).astype(BF16)

    cw, cd = {}, {}

    def share_group(name, g):
        place_tile(w.at[g])
        cw[name] = [
            send(w.at[g, rows, :], wo.at[g, rows, :], cpartner)
            for rows in (pl.ds(0, 112), pl.ds(UP0, 96))
        ]

    def forward_group(name, g):
        @pl.loop(0, 2)
        def _(r):
            rows = pl.ds(pl.multiple_of(r * ROWS, ROWS), ROWS)
            both = lax.dot_general(
                tok[rows, :], w[g], (((1,), (1,)), ((), ())), preferred_element_type=F32
            )
            gate, up = both[:, 0:128], both[:, 128:256]
            grad_in = cotp[g, rows, :].astype(F32)
            sig = jax.nn.sigmoid(gate)
            active = gate * sig
            hid[rows, pl.ds(pl.multiple_of(g * 128, 128), 128)] = (active * up).astype(BF16)
            d_gate = (grad_in * up * sig * (1.0 + gate * (1.0 - sig))).astype(BF16)
            d_up = (grad_in * active).astype(BF16)
            half = pl.ds(pl.multiple_of(r * 8, 8), 8)
            for k, part in ((0, d_gate), (1, d_up)):
                part4 = part.reshape(8, 2, 32, 128)
                for c in range(2):
                    d[g, c, half, :, k * 128 : (k + 1) * 128] = part4[:, c]
                dt[name, k * 128 : (k + 1) * 128, rows] = part.T

        cd[name] = send(d.at[g, 1 - core], do.at[g], cpartner)

    def token_terms(groups, begin, k):
        half = pl.ds(pl.multiple_of((1 - xl, xl)[k] * 8, 8), 8)

        @pl.loop(0, 5)
        def _(n):
            cols = pl.ds(pl.multiple_of(n * 512, 512), 512)
            terms = [] if begin else [ig[half, :, cols].reshape(256, 512)]
            for g in groups:
                for left, right in ((d.at[g, core], w.at[g]), (do.at[g], wo.at[g])):
                    terms.append(
                        jnp.dot(
                            left[half].reshape(256, 256), right[:, cols],
                            preferred_element_type=F32,
                        )
                    )
            ig[half, :, cols] = functools.reduce(jnp.add, terms).reshape(8, 32, 512)

    def put_grads(name, dst, h, kind):
        cols = pl.ds(h * HALF, HALF)
        part = jnp.dot(dt[name], tok[:, cols], preferred_element_type=F32)
        dst[0:96, cols] = part[0:96].astype(kind)
        dst[96:112, cols] = jnp.concatenate([part[96:104], part[224:232]], axis=0).astype(kind)
        dst[112:208, cols] = part[128:224].astype(kind)

    def core_wait(name, g):
        for copy in cw[name]:
            copy.wait_recv()
        place_tile(wo.at[g])
        cd[name].wait_recv()

    RIGHT, LEFT, FAR, OWN = range(4)
    share_group(OWN, y)
    forward_group(OWN, y)
    cross(2)
    shared[0].wait_recv()
    ref = w.at[yl, 96:112, :]
    onward = send(ref, ref, right_y)

    early = {}
    for dirn, name, g in ((0, LEFT, yl), (1, RIGHT, yr)):
        for kind in range(2):
            for part in range(3):
                ot[kind, part, dirn].wait_recv()
                if kind != dirn:
                    own[kind, part, dirn].wait_recv()
        if dirn == 1:
            shared[1].wait_recv()
        share_group(name, g)
        forward_group(name, g)
        to, h = (1, 0) if dirn == 0 else (0, 1)
        put_grads(name, dwb.at[name], h, BF16)
        early[to] = send(dwb.at[name, :, pl.ds(h * HALF, HALF)], ra.at[to], ydir[to])

    for kind in range(2):
        for part in range(3):
            x2[kind, part].wait_recv()
    onward.wait_recv()
    share_group(FAR, yo)
    forward_group(FAR, yo)
    core_wait(OWN, y)
    core_wait(LEFT, yl)
    core_wait(RIGHT, yr)
    for k in range(2):
        token_terms((y, yl, yr), True, k)
    core_wait(FAR, yo)

    zc = {}

    def z_step(step, k):
        c = (1 - xl, xl)[k]
        for dirn in range(2):
            owner = (z + (5 - step)) % NZ if dirn == 0 else (z + NZ - (5 - step)) % NZ
            row = c * 8 + owner
            if step == 1:
                cols = pl.ds(dirn * HALF, HALF)
                zs[dirn, 0, k, :, cols] = ig[row, :, cols].astype(BF16)
                zc[1, k, dirn] = send(
                    zs.at[dirn, 0, k, :, cols], zr.at[dirn, 0, k, :, cols], zdir[dirn]
                )
                continue
            zc[step - 1, k, dirn].wait_recv()
            for h in range(2):
                cols = pl.ds(h * HALF, HALF)
                term = ig[row, :, cols]
                if step > 2 or h == dirn:
                    term = term + zr[dirn, step - 2, k, :, cols].astype(F32)
                zs[dirn, step - 1, k, :, cols] = term.astype(BF16)
            zc[step, k, dirn] = send(zs.at[dirn, step - 1, k], zr.at[dirn, step - 1, k], zdir[dirn])

    for k in range(2):
        token_terms((yo,), False, k)
        z_step(1, k)

    gate_own = pl.ds(pl.multiple_of(MAIN * xh, 16), MAIN)
    gate_ot = pl.ds(pl.multiple_of(MAIN * other, 16), MAIN)
    up_own = pl.ds(pl.multiple_of(112 + MAIN * xh, 16), MAIN)
    up_ot = pl.ds(pl.multiple_of(112 + MAIN * other, 16), MAIN)
    tile = pl.ds(96, TILE)

    def columns(h, q):
        return pl.ds(h * HALF + q * WIDE, WIDE)

    across, far, second_hop, xc = {}, {}, {}, {}
    for h in range(2):
        put_grads(FAR, dwb.at[FAR], h, BF16)
        for q in range(CROSS, PIECES):
            far[h, q] = send(dwb.at[FAR, :, columns(h, q)], rb.at[h, q], ydir[h])
    for q in range(CROSS):
        for h in range(2):
            across[h, q] = [
                send(dwb.at[FAR, gate_ot, columns(h, q)], rx.at[h, q, 0:MAIN, :], xpartner),
                send(dwb.at[FAR, up_ot, columns(h, q)], rx.at[h, q, MAIN : 2 * MAIN, :], xpartner),
            ]
    put_grads(LEFT, dwb.at[LEFT], 1, BF16)
    put_grads(RIGHT, dwb.at[RIGHT], 0, BF16)
    put_grads(OWN, dwown, 0, F32)
    put_grads(OWN, dwown, 1, F32)

    def join(q):
        for h in range(2):
            for copy in across[h, q]:
                copy.wait_recv()
            cols = columns(h, q)
            for rows, begin in ((gate_own, 0), (up_own, MAIN)):
                sb[h, q, begin : begin + MAIN, :] = (
                    dwb[FAR, rows, cols].astype(F32) + rx[h, q, begin : begin + MAIN, :].astype(F32)
                ).astype(BF16)
            sb[h, q, 2 * MAIN :, :] = dwb[FAR, tile, cols]
            far[h, q] = send(sb.at[h, q], rb.at[h, q, 0:112, :], ydir[h])

    def pass_on(q):
        for h in range(2):
            far[h, q].wait_recv()
            cols = columns(h, q)
            if q < CROSS:
                parts = ((gate_own, 0, MAIN), (up_own, MAIN, MAIN), (tile, 2 * MAIN, TILE))
            else:
                parts = ((pl.ds(0, PAY), 0, PAY),)
            for rows, begin, n in parts:
                dwb[h, rows, cols] = (
                    dwb[h, rows, cols].astype(F32) + rb[h, q, begin : begin + n, :].astype(F32)
                ).astype(BF16)
            second_hop[h, q] = send(dwb.at[h, :, cols], rc.at[h, q], ydir[h])

    def collect(q):
        for h in range(2):
            second_hop[h, q].wait_recv()
            if q == CROSS:
                early[1 - h].wait_recv()
            cols = columns(h, q)
            here = pl.ds(q * WIDE, WIDE)

            def summed(rows):
                return (
                    dwown[rows, cols]
                    + rc[h, q, rows, :].astype(F32)
                    + ra[1 - h, rows, here].astype(F32)
                )

            xs2[h, q, 0:MAIN, :] = summed(gate_ot).astype(BF16)
            xs2[h, q, MAIN : 2 * MAIN, :] = summed(up_ot).astype(BF16)
            both = summed(tile)
            xs2[h, q, 2 * MAIN :, :] = both.astype(BF16)
            xc[h, q] = send(xs2.at[h, q], xr2.at[h, q], xpartner)
            fin[0:MAIN, cols] = summed(gate_own)
            fin[MAIN : 2 * MAIN, cols] = summed(up_own)
            fin[2 * MAIN :, cols] = both

    def finish(q):
        scale = 1.0 / math.sqrt(TOK * NY * NXH)
        for h in range(2):
            xc[h, q].wait_recv()
            cols = columns(h, q)
            ucols = pl.ds(D + h * HALF + q * WIDE, WIDE)
            fin[:, cols] = (fin[:, cols] + xr2[h, q].astype(F32)) * scale
            for j in range(PAGES):
                p = idx[3, j]
                rest = 2 * MAIN + 2 * xh + p - MAIN
                row = jnp.where(p < MAIN, p, rest)
                urow = jnp.where(p < MAIN, MAIN + p, rest + 8)
                out_grads[j, :, cols] = fin[pl.ds(row, 1), cols]
                out_grads[j, :, ucols] = fin[pl.ds(urow, 1), cols]

    def z_total(k):
        row = (1 - xl, xl)[k] * 8 + z
        for dirn in range(2):
            zc[4, k, dirn].wait_recv()
        return ig[row] + zr[0, 3, k].astype(F32) + zr[1, 3, k].astype(F32)

    z_step(2, 0)
    z_step(2, 1)
    join(0)
    pass_on(2)
    join(1)
    pass_on(3)
    z_step(3, 0)
    collect(2)
    pass_on(4)
    for r in range(2):
        rows = pl.ds(r * ROWS, ROWS)
        out_hidden[:, rows] = lax.dot_general(
            matrix(), hid[rows, :], (((1,), (1,)), ((), ())), preferred_element_type=F32
        ).astype(BF16)
    pass_on(0)
    z_step(3, 1)
    pass_on(1)
    collect(3)
    finish(2)
    z_step(4, 0)
    collect(4)
    finish(3)
    collect(0)
    z_step(4, 1)
    finish(4)
    collect(1)
    finish(0)
    ls[...] = z_total(0).astype(BF16)
    lcopy = send(ls, lr, lpartner)
    finish(1)
    own_sum = z_total(1)
    lcopy.wait_recv()
    out_ig[...] = (own_sum + lr[...].astype(F32)).astype(BF16)

    for copy in started:
        copy.wait_send()


def hand_over(*refs):
    ins, outs, held, (arrive, leave) = refs[0:4], refs[4:8], refs[8:12], refs[12:14]
    reads = [pltpu.make_async_copy(ins[i], held[i], arrive.at[i]) for i in range(4)]
    writes = [pltpu.make_async_copy(held[i], outs[i], leave.at[i]) for i in range(4)]
    for copy in reads:
        copy.start()
    for read, write in zip(reads, writes):
        read.wait()
        write.start()
    for copy in writes:
        copy.wait()


def body(tokens, masters, cotangent, partner, slots):
    vmem = pl.BlockSpec(memory_space=pltpu.VMEM)
    outs = pl.pallas_call(
        kernel,
        out_shape=(
            jax.ShapeDtypeStruct((PAGES, 1, 2 * D), F32),
            jax.ShapeDtypeStruct((UNITS, TOK), BF16),
            jax.ShapeDtypeStruct((32, D), BF16),
            jax.ShapeDtypeStruct((PAGES, 1, 2 * D), F32),
        ),
        in_specs=[
            vmem,
            vmem,
            vmem,
            pl.BlockSpec(memory_space=pl.ANY),
            pl.BlockSpec(memory_space=pl.ANY),
        ],
        out_specs=(vmem,) * 4,
        scratch_shapes=[
            pltpu.VMEM((8, 128), jnp.int32),
            pltpu.SMEM((8, 128), jnp.int32),
            pltpu.VMEM((1, LANES), jnp.int32),
            pltpu.VMEM((TOK, D), BF16),
            pltpu.VMEM((UNITS, TOK), BF16),
            pltpu.VMEM((NY, TOK, 128), BF16),
            pltpu.VMEM((TOK, LANES), BF16),
            pltpu.VMEM((SHARDS, 1, 2 * D), F32),
            pltpu.VMEM((SHARDS, 1, 2 * D), F32),
            pltpu.VMEM((PAGES + 6, 2 * D), F32),
            pltpu.VMEM((TILE, D), BF16),
            pltpu.VMEM((TILE, D), BF16),
            pltpu.VMEM((NY, 256, D), BF16),
            pltpu.VMEM((NY, 256, D), BF16),
            pltpu.VMEM((NY, 2, 16, 32, 256), BF16),
            pltpu.VMEM((NY, 16, 32, 256), BF16),
            pltpu.VMEM((4, 256, TOK), BF16),
            pltpu.VMEM((3, PAY, D), BF16),
            pltpu.VMEM((PAY, D), F32),
            pltpu.VMEM((2, PAY, HALF), BF16),
            pltpu.VMEM((2, CROSS, 2 * MAIN, WIDE), BF16),
            pltpu.VMEM((2, CROSS, 112, WIDE), BF16),
            pltpu.VMEM((2, PIECES, PAY, WIDE), BF16),
            pltpu.VMEM((2, PIECES, PAY, WIDE), BF16),
            pltpu.VMEM((112, D), F32),
            pltpu.VMEM((2, PIECES, 112, WIDE), BF16),
            pltpu.VMEM((2, PIECES, 112, WIDE), BF16),
            pltpu.VMEM((16, 32, D), F32),
            pltpu.VMEM((2, 4, 2, 32, D), BF16),
            pltpu.VMEM((2, 4, 2, 32, D), BF16),
            pltpu.VMEM((32, D), BF16),
            pltpu.VMEM((32, D), BF16),
            pltpu.SemaphoreType.DMA((SHARDS,)),
            pltpu.SemaphoreType.DMA((SHARDS,)),
            pltpu.SemaphoreType.DMA((N_SENDS,)),
            pltpu.SemaphoreType.DMA((N_SENDS,)),
            pltpu.SemaphoreType.DMA((3,)),
        ],
        compiler_params=pltpu.CompilerParams(
            collective_id=0, has_side_effects=True, vmem_limit_bytes=60 * 2**20
        ),
    )(partner, slots, jnp.transpose(masters, (1, 0, 2)), tokens, cotangent.T)
    new, hidden, input_grad, grads = pl.pallas_call(
        hand_over,
        out_shape=tuple(jax.ShapeDtypeStruct(out.shape, out.dtype) for out in outs),
        in_specs=[pl.BlockSpec(memory_space=pl.ANY)] * 4,
        out_specs=(pl.BlockSpec(memory_space=pl.ANY),) * 4,
        scratch_shapes=[pltpu.VMEM(out.shape, out.dtype) for out in outs]
        + [pltpu.SemaphoreType.DMA((4,))] * 2,
    )(*outs)
    return (
        jnp.transpose(new, (1, 0, 2)),
        hidden.T,
        input_grad,
        jnp.transpose(grads, (1, 0, 2)),
    )


def solution(mesh):
    in_specs = (P("dp", None), P("dp", "shard", None), P("dp", "shard"), P(), P())
    out_specs = (
        P("dp", "shard", None),
        P("dp", "shard"),
        P(("dp", "shard"), None),
        P("dp", "shard", None),
    )
    return jax.shard_map(body, mesh=mesh, in_specs=in_specs, out_specs=out_specs, check_vma=False)
```

```python
import functools
import math

import jax
import jax.numpy as jnp
from jax import lax
from jax.experimental import pallas as pl
from jax.experimental.pallas import tpu as pltpu
from jax.sharding import PartitionSpec as P

MESH = pl.DeviceIdType.MESH
F32, BF16 = jnp.float32, jnp.bfloat16

NY, NXH, NXL, NZ, NC = 4, 2, 2, 8, 2
SHARDS = NXL * NZ * NC
MOVED = SHARDS - 1
PAGES = 50
KEPT = PAGES - MOVED
UNITS = NY * NXH * PAGES
D = 2560
TOK = 1024
HALF = D // 2
PIECES = 5
WIDE = HALF // PIECES
CROSS = 2
PART = 16
FIRST = 2 * PART - KEPT
MAIN = 48
TILE = 16
PAY = 4 * MAIN + TILE
UP0 = 128
ROWS = TOK // 2
LANES = NY * 128
N_SENDS = 128


def total(mask, value, axis):
    return jnp.sum(jnp.where(mask, value, 0), axis=axis, keepdims=True)


def peer_at(me, k, sign):
    turn, rest = k // 4, k % 4
    ahead = (turn % 2) * ((turn + 1) // 2) + (1 - turn % 2) * ((NZ - turn // 2) % NZ)
    xl, z, core = me // 16, (me // 2) % NZ, me % 2
    z = (z + sign * ahead + NZ) % NZ
    return ((xl + rest // 2) % NXL) * 16 + z * 2 + (core + rest % 2) % NC


def plan(me, partner, slots, table, source):
    def iota(shape, axis):
        return lax.broadcasted_iota(jnp.int32, shape, axis)

    mine = iota((MOVED, SHARDS), 1) == me
    peer_c, slot_c = total(mine, partner[...], 1), total(mine, slots[...], 1)
    sub, lane = iota((MOVED, 128), 0), iota((MOVED, 128), 1)
    peer_r, slot_r = total(sub == lane, peer_c, 0), total(sub == lane, slot_c, 0)
    give_r = total(lane == peer_c, slot_c, 0)
    take_r = total(lane == slot_c, peer_c + 1, 0) - 1
    sub, lane = iota((64, 128), 0), iota((64, 128), 1)
    take_c = total((sub == slot_r) & (lane < MOVED), peer_r + 1, 1) - 1

    def place(take, before):
        ahead = (take // 2) % NZ - (me // 2) % NZ
        ahead = jnp.where(ahead < 0, ahead + NZ, ahead)
        turn = jnp.where(ahead == 0, 0, jnp.where(ahead < 5, 2 * ahead - 1, 2 * (NZ - ahead)))
        side = jnp.where(take // 16 == me // 16, 0, 2) + jnp.where(take % 2 == me % 2, 0, 1)
        return jnp.where(take < 0, before, KEPT + 4 * turn + side - 1)

    place_r = place(take_r, total((take_c < 0) & (sub < PAGES) & (sub < lane), 1, 0))
    place_c = place(take_c, total((take_r < 0) & (lane < PAGES) & (lane < sub), 1, 1))
    order_r = total((place_c == lane) & (sub < PAGES), sub, 0)
    for i, row in enumerate((give_r, take_r, order_r, place_r)):
        table[i : i + 1, :] = row
    lane = iota((1, LANES), 1)
    group = lane // 128
    lane = lane - group * 128
    at = jnp.where(lane < 2 * MAIN, lane % MAIN, jnp.where(lane < 100, MAIN + lane % 2, -1))
    block = jnp.where(lane < 2 * MAIN, lane // MAIN, (lane - 2 * MAIN) // 2)
    sub = iota((64, LANES), 0)
    unit = total((place_c == at) & (sub < PAGES), sub, 0)
    source[...] = jnp.where(at < 0, -1, group * (2 * PAGES) + block * PAGES + unit)


def kernel(
    partner, slots, masters, tokens_hbm, cot_hbm,
    out_masters, out_hidden, out_ig, out_grads,
    table, idx, source, tok, cot, cotp, hid, outgoing, incoming, stage, tx, tr, w, wo, d, do, dt, dwb, dwown,
    ra, rx, sb, rb, rc, fin, xs2, xr2, ig, zs, zr, ls, lr,
    psend, precv, ssem, rsem, lsem,
):
    dp = lax.axis_index("dp")
    me = lax.axis_index("shard")
    y, xh = dp // 2, dp % 2
    xl, z, core = me // 16, (me // 2) % 8, me % 2
    yr, yl, yo = (y + 1) % NY, (y + NY - 1) % NY, (y + 2) % NY
    right_y = (yr * 2 + xh, me)
    left_y = (yl * 2 + xh, me)
    xpartner = (y * 2 + 1 - xh, me)
    cpartner = (dp, me + 1 - 2 * core)
    lpartner = (dp, (1 - xl) * 16 + z * 2 + core)
    right_z = (dp, xl * 16 + ((z + 1) % NZ) * 2 + core)
    left_z = (dp, xl * 16 + ((z + NZ - 1) % NZ) * 2 + core)
    ydir = (right_y, left_y)
    zdir = (right_z, left_z)

    count = [0]
    started = []

    def send(src, dst, device):
        n = count[0]
        count[0] += 1
        copy = pltpu.make_async_remote_copy(
            src_ref=src, dst_ref=dst, send_sem=ssem.at[n], recv_sem=rsem.at[n],
            device_id=device, device_id_type=MESH,
        )
        copy.start()
        started.append(copy)
        return copy

    load_tok = pltpu.make_async_copy(tokens_hbm, tok, lsem.at[0])
    load_cot = pltpu.make_async_copy(cot_hbm, cot, lsem.at[1])
    load_cot.start()
    load_tok.start()

    barrier = pltpu.get_barrier_semaphore()
    for peer in (right_y, left_y, xpartner):
        pl.semaphore_signal(barrier, inc=1, device_id=peer, device_id_type=MESH)

    def greet(k, carry):
        pl.semaphore_signal(
            barrier, inc=1, device_id=(dp, (me + k) % SHARDS), device_id_type=MESH
        )
        return carry

    lax.fori_loop(1, SHARDS, greet, 0)
    plan(me, partner, slots, table, source)
    load_idx = pltpu.make_async_copy(table, idx, lsem.at[2])
    load_idx.start()
    incoming[me] = jnp.zeros((1, 2 * D), F32)
    load_idx.wait()

    def page_fill(k, carry):
        t = peer_at(me, k, -1)
        outgoing[t] = masters[idx[0, t]]
        return carry

    lax.fori_loop(1, SHARDS, page_fill, 0)

    def at(kind, b, part):
        return pl.multiple_of(kind * UP0 + MAIN * b + PART * part, 16)

    def span(g, kind, b, part):
        return w.at[g, pl.ds(at(kind, b, part), PART), :]

    def put_block(part):
        begin = PART * part
        for kind in range(2):
            w[y, pl.ds(at(kind, xh, part), PART), :] = stage[
                begin : begin + PART, kind * D : (kind + 1) * D
            ].astype(BF16)

    for i in range(PART):
        stage[i : i + 1, :] = masters[idx[2, i]]

    pl.semaphore_wait(barrier, 3 + SHARDS - 1)

    def page_out(k, carry):
        t = peer_at(me, k, -1)
        pltpu.make_async_remote_copy(
            src_ref=outgoing.at[t], dst_ref=incoming.at[me],
            send_sem=psend.at[t], recv_sem=precv.at[me],
            device_id=(dp, t), device_id_type=MESH,
        ).start()
        return carry

    other = 1 - xh
    xa, own, ot, fwd, x2 = {}, {}, {}, {}, {}

    def spread(table, kind, b, part):
        for dirn in range(2):
            ref = span(y, kind, b, part)
            table[kind, part, dirn] = send(ref, ref, ydir[dirn])

    def give_x(part):
        for kind in range(2):
            ref = span(y, kind, xh, part)
            xa[kind, part] = send(ref, ref, xpartner)

    def take_x(part):
        for kind in range(2):
            xa[kind, part].wait_recv()
            spread(ot, kind, other, part)

    def forward_on(part):
        for kind in range(2):
            own[kind, part, kind].wait_recv()
            ref = span((yl, yr)[kind], kind, xh, part)
            fwd[kind, part] = send(ref, ref, ydir[kind])

    def cross(part):
        for kind in range(2):
            fwd[kind, part].wait_recv()
            ref = span(yo, kind, xh, part)
            x2[kind, part] = send(ref, ref, xpartner)

    def own_out(part):
        put_block(part)
        give_x(part)
        for kind in range(2):
            spread(own, kind, xh, part)

    lax.fori_loop(1, SHARDS, page_out, 0)
    own_out(0)
    for g in range(NY):
        for ref in (w, wo):
            ref[g, 112:128, :] = jnp.zeros((16, D), BF16)
            ref[g, 240:256, :] = jnp.zeros((16, D), BF16)

    def matrix():
        unit = lax.broadcasted_iota(jnp.int32, (UNITS, LANES), 0)
        return jnp.where(unit == source[...], 1.0, 0.0).astype(BF16)

    def page_wait(k, carry):
        t = peer_at(me, k, 1)
        pltpu.make_async_remote_copy(
            src_ref=outgoing.at[t], dst_ref=incoming.at[t],
            send_sem=psend.at[t], recv_sem=precv.at[t],
            device_id=(dp, t), device_id_type=MESH,
        ).wait()
        return carry

    def pages_in(begin, end):
        lax.fori_loop(begin + 1, end + 1, page_wait, 0)
        for k in range(begin, end):
            stage[KEPT + k : KEPT + k + 1, :] = incoming[peer_at(me, k + 1, 1)]

    for i in range(PART, KEPT):
        stage[i : i + 1, :] = masters[idx[2, i]]
    take_x(0)
    forward_on(0)
    load_cot.wait()
    for r in range(2):
        rows = pl.ds(r * ROWS, ROWS)
        moved = lax.dot_general(
            cot[:, rows], matrix(), (((0,), (0,)), ((), ())), preferred_element_type=F32
        ).astype(BF16)
        for g in range(NY):
            cotp[g, rows, :] = moved[:, g * 128 : (g + 1) * 128]
    load_tok.wait()
    pages_in(0, FIRST)
    own_out(1)
    take_x(1)
    forward_on(1)
    pages_in(FIRST, MOVED)
    own_out(2)
    none = jnp.zeros((6, D), F32)
    last = stage[MAIN:PAGES, :]
    tx[...] = jnp.concatenate([last[:, 0:D], none, last[:, D:], none], axis=0).astype(BF16)
    tcopy = send(tx, tr, xpartner)
    cross(0)
    cross(1)

    for j in range(PAGES):
        p = idx[1, j]
        out_masters[j] = jnp.where(p < 0, masters[j], incoming[jnp.maximum(p, 0)])

    take_x(2)
    forward_on(2)
    tcopy.wait_recv()
    mine, theirs = tx[...].astype(F32), tr[...].astype(F32)
    first = jnp.where(xh == 0, mine, theirs)
    second = jnp.where(xh == 0, theirs, mine)
    none4 = jnp.zeros((4, D), F32)
    w[y, 96:112, :] = jnp.concatenate(
        [first[0:2], second[0:2], none4, first[8:10], second[8:10], none4], axis=0
    ).astype(BF16)
    shared = {}
    for dirn in range(2):
        ref = w.at[y, 96:112, :]
        shared[dirn] = send(ref, ref, ydir[dirn])

    def place_tile(ref):
        t = ref[96:112, :].astype(F32)
        ref[224:240, :] = jnp.concatenate([t[8:16], t[0:8]], axis=0).astype(BF16)

    cw, cd = {}, {}

    def share_group(name, g):
        place_tile(w.at[g])
        cw[name] = [
            send(w.at[g, rows, :], wo.at[g, rows, :], cpartner)
            for rows in (pl.ds(0, 112), pl.ds(UP0, 96))
        ]

    def forward_group(name, g):
        @pl.loop(0, 2)
        def _(r):
            rows = pl.ds(pl.multiple_of(r * ROWS, ROWS), ROWS)
            both = lax.dot_general(
                tok[rows, :], w[g], (((1,), (1,)), ((), ())), preferred_element_type=F32
            )
            gate, up = both[:, 0:128], both[:, 128:256]
            grad_in = cotp[g, rows, :].astype(F32)
            sig = jax.nn.sigmoid(gate)
            active = gate * sig
            hid[rows, pl.ds(pl.multiple_of(g * 128, 128), 128)] = (active * up).astype(BF16)
            d_gate = (grad_in * up * sig * (1.0 + gate * (1.0 - sig))).astype(BF16)
            d_up = (grad_in * active).astype(BF16)
            half = pl.ds(pl.multiple_of(r * 8, 8), 8)
            for k, part in ((0, d_gate), (1, d_up)):
                part4 = part.reshape(8, 2, 32, 128)
                for c in range(2):
                    d[g, c, half, :, k * 128 : (k + 1) * 128] = part4[:, c]
                dt[name, k * 128 : (k + 1) * 128, rows] = part.T

        cd[name] = send(d.at[g, 1 - core], do.at[g], cpartner)

    def token_terms(groups, begin, k):
        half = pl.ds(pl.multiple_of((1 - xl, xl)[k] * 8, 8), 8)

        @pl.loop(0, 5)
        def _(n):
            cols = pl.ds(pl.multiple_of(n * 512, 512), 512)
            terms = [] if begin else [ig[half, :, cols].reshape(256, 512)]
            for g in groups:
                for left, right in ((d.at[g, core], w.at[g]), (do.at[g], wo.at[g])):
                    terms.append(
                        jnp.dot(
                            left[half].reshape(256, 256), right[:, cols],
                            preferred_element_type=F32,
                        )
                    )
            ig[half, :, cols] = functools.reduce(jnp.add, terms).reshape(8, 32, 512)

    def put_grads(name, dst, h, kind):
        cols = pl.ds(h * HALF, HALF)
        part = jnp.dot(dt[name], tok[:, cols], preferred_element_type=F32)
        dst[0:96, cols] = part[0:96].astype(kind)
        dst[96:112, cols] = jnp.concatenate([part[96:104], part[224:232]], axis=0).astype(kind)
        dst[112:208, cols] = part[128:224].astype(kind)

    def core_wait(name, g):
        for copy in cw[name]:
            copy.wait_recv()
        place_tile(wo.at[g])
        cd[name].wait_recv()

    RIGHT, LEFT, FAR, OWN = range(4)
    share_group(OWN, y)
    forward_group(OWN, y)
    cross(2)
    shared[0].wait_recv()
    ref = w.at[yl, 96:112, :]
    onward = send(ref, ref, right_y)

    early = {}
    for dirn, name, g in ((0, LEFT, yl), (1, RIGHT, yr)):
        for kind in range(2):
            for part in range(3):
                ot[kind, part, dirn].wait_recv()
                if kind != dirn:
                    own[kind, part, dirn].wait_recv()
        if dirn == 1:
            shared[1].wait_recv()
        share_group(name, g)
        forward_group(name, g)
        to, h = (1, 0) if dirn == 0 else (0, 1)
        put_grads(name, dwb.at[name], h, BF16)
        early[to] = send(dwb.at[name, :, pl.ds(h * HALF, HALF)], ra.at[to], ydir[to])

    for kind in range(2):
        for part in range(3):
            x2[kind, part].wait_recv()
    onward.wait_recv()
    share_group(FAR, yo)
    forward_group(FAR, yo)
    core_wait(OWN, y)
    core_wait(LEFT, yl)
    core_wait(RIGHT, yr)
    for k in range(2):
        token_terms((y, yl, yr), True, k)
    core_wait(FAR, yo)

    zc = {}

    def z_step(step, k):
        c = (1 - xl, xl)[k]
        for dirn in range(2):
            owner = (z + (5 - step)) % NZ if dirn == 0 else (z + NZ - (5 - step)) % NZ
            row = c * 8 + owner
            if step == 1:
                cols = pl.ds(dirn * HALF, HALF)
                zs[dirn, 0, k, :, cols] = ig[row, :, cols].astype(BF16)
                zc[1, k, dirn] = send(
                    zs.at[dirn, 0, k, :, cols], zr.at[dirn, 0, k, :, cols], zdir[dirn]
                )
                continue
            zc[step - 1, k, dirn].wait_recv()
            for h in range(2):
                cols = pl.ds(h * HALF, HALF)
                term = ig[row, :, cols]
                if step > 2 or h == dirn:
                    term = term + zr[dirn, step - 2, k, :, cols].astype(F32)
                zs[dirn, step - 1, k, :, cols] = term.astype(BF16)
            zc[step, k, dirn] = send(zs.at[dirn, step - 1, k], zr.at[dirn, step - 1, k], zdir[dirn])

    for k in range(2):
        token_terms((yo,), False, k)
        z_step(1, k)

    gate_own = pl.ds(pl.multiple_of(MAIN * xh, 16), MAIN)
    gate_ot = pl.ds(pl.multiple_of(MAIN * other, 16), MAIN)
    up_own = pl.ds(pl.multiple_of(112 + MAIN * xh, 16), MAIN)
    up_ot = pl.ds(pl.multiple_of(112 + MAIN * other, 16), MAIN)
    tile = pl.ds(96, TILE)

    def columns(h, q):
        return pl.ds(h * HALF + q * WIDE, WIDE)

    across, far, second_hop, xc = {}, {}, {}, {}
    for h in range(2):
        put_grads(FAR, dwb.at[FAR], h, BF16)
        for q in range(CROSS, PIECES):
            far[h, q] = send(dwb.at[FAR, :, columns(h, q)], rb.at[h, q], ydir[h])
    for q in range(CROSS):
        for h in range(2):
            across[h, q] = [
                send(dwb.at[FAR, gate_ot, columns(h, q)], rx.at[h, q, 0:MAIN, :], xpartner),
                send(dwb.at[FAR, up_ot, columns(h, q)], rx.at[h, q, MAIN : 2 * MAIN, :], xpartner),
            ]
    put_grads(LEFT, dwb.at[LEFT], 1, BF16)
    put_grads(RIGHT, dwb.at[RIGHT], 0, BF16)
    put_grads(OWN, dwown, 0, F32)
    put_grads(OWN, dwown, 1, F32)

    def join(q):
        for h in range(2):
            for copy in across[h, q]:
                copy.wait_recv()
            cols = columns(h, q)
            for rows, begin in ((gate_own, 0), (up_own, MAIN)):
                sb[h, q, begin : begin + MAIN, :] = (
                    dwb[FAR, rows, cols].astype(F32) + rx[h, q, begin : begin + MAIN, :].astype(F32)
                ).astype(BF16)
            sb[h, q, 2 * MAIN :, :] = dwb[FAR, tile, cols]
            far[h, q] = send(sb.at[h, q], rb.at[h, q, 0:112, :], ydir[h])

    def pass_on(q):
        for h in range(2):
            far[h, q].wait_recv()
            cols = columns(h, q)
            if q < CROSS:
                parts = ((gate_own, 0, MAIN), (up_own, MAIN, MAIN), (tile, 2 * MAIN, TILE))
            else:
                parts = ((pl.ds(0, PAY), 0, PAY),)
            for rows, begin, n in parts:
                dwb[h, rows, cols] = (
                    dwb[h, rows, cols].astype(F32) + rb[h, q, begin : begin + n, :].astype(F32)
                ).astype(BF16)
            second_hop[h, q] = send(dwb.at[h, :, cols], rc.at[h, q], ydir[h])

    def collect(q):
        for h in range(2):
            second_hop[h, q].wait_recv()
            if q == CROSS:
                early[1 - h].wait_recv()
            cols = columns(h, q)
            here = pl.ds(q * WIDE, WIDE)

            def summed(rows):
                return (
                    dwown[rows, cols]
                    + rc[h, q, rows, :].astype(F32)
                    + ra[1 - h, rows, here].astype(F32)
                )

            xs2[h, q, 0:MAIN, :] = summed(gate_ot).astype(BF16)
            xs2[h, q, MAIN : 2 * MAIN, :] = summed(up_ot).astype(BF16)
            both = summed(tile)
            xs2[h, q, 2 * MAIN :, :] = both.astype(BF16)
            xc[h, q] = send(xs2.at[h, q], xr2.at[h, q], xpartner)
            fin[0:MAIN, cols] = summed(gate_own)
            fin[MAIN : 2 * MAIN, cols] = summed(up_own)
            fin[2 * MAIN :, cols] = both

    def finish(q):
        scale = 1.0 / math.sqrt(TOK * NY * NXH)
        for h in range(2):
            xc[h, q].wait_recv()
            cols = columns(h, q)
            ucols = pl.ds(D + h * HALF + q * WIDE, WIDE)
            fin[:, cols] = (fin[:, cols] + xr2[h, q].astype(F32)) * scale
            for j in range(PAGES):
                p = idx[3, j]
                rest = 2 * MAIN + 2 * xh + p - MAIN
                row = jnp.where(p < MAIN, p, rest)
                urow = jnp.where(p < MAIN, MAIN + p, rest + 8)
                out_grads[j, :, cols] = fin[pl.ds(row, 1), cols]
                out_grads[j, :, ucols] = fin[pl.ds(urow, 1), cols]

    def z_total(k):
        row = (1 - xl, xl)[k] * 8 + z
        for dirn in range(2):
            zc[4, k, dirn].wait_recv()
        return ig[row] + zr[0, 3, k].astype(F32) + zr[1, 3, k].astype(F32)

    z_step(2, 0)
    z_step(2, 1)
    join(0)
    pass_on(2)
    join(1)
    pass_on(3)
    z_step(3, 0)
    collect(2)
    pass_on(4)
    for r in range(2):
        rows = pl.ds(r * ROWS, ROWS)
        out_hidden[:, rows] = lax.dot_general(
            matrix(), hid[rows, :], (((1,), (1,)), ((), ())), preferred_element_type=F32
        ).astype(BF16)
    pass_on(0)
    z_step(3, 1)
    pass_on(1)
    collect(3)
    finish(2)
    z_step(4, 0)
    collect(4)
    finish(3)
    collect(0)
    z_step(4, 1)
    finish(4)
    collect(1)
    finish(0)
    ls[...] = z_total(0).astype(BF16)
    lcopy = send(ls, lr, lpartner)
    finish(1)
    own_sum = z_total(1)
    lcopy.wait_recv()
    out_ig[...] = (own_sum + lr[...].astype(F32)).astype(BF16)

    for copy in started:
        copy.wait_send()


def hand_over(*refs):
    ins, outs, held, (arrive, leave) = refs[0:4], refs[4:8], refs[8:12], refs[12:14]
    reads = [pltpu.make_async_copy(ins[i], held[i], arrive.at[i]) for i in range(4)]
    writes = [pltpu.make_async_copy(held[i], outs[i], leave.at[i]) for i in range(4)]
    for copy in reads:
        copy.start()
    for read, write in zip(reads, writes):
        read.wait()
        write.start()
    for copy in writes:
        copy.wait()


def body(tokens, masters, cotangent, partner, slots):
    vmem = pl.BlockSpec(memory_space=pltpu.VMEM)
    outs = pl.pallas_call(
        kernel,
        out_shape=(
            jax.ShapeDtypeStruct((PAGES, 1, 2 * D), F32),
            jax.ShapeDtypeStruct((UNITS, TOK), BF16),
            jax.ShapeDtypeStruct((32, D), BF16),
            jax.ShapeDtypeStruct((PAGES, 1, 2 * D), F32),
        ),
        in_specs=[
            vmem,
            vmem,
            vmem,
            pl.BlockSpec(memory_space=pl.ANY),
            pl.BlockSpec(memory_space=pl.ANY),
        ],
        out_specs=(vmem,) * 4,
        scratch_shapes=[
            pltpu.VMEM((8, 128), jnp.int32),
            pltpu.SMEM((8, 128), jnp.int32),
            pltpu.VMEM((1, LANES), jnp.int32),
            pltpu.VMEM((TOK, D), BF16),
            pltpu.VMEM((UNITS, TOK), BF16),
            pltpu.VMEM((NY, TOK, 128), BF16),
            pltpu.VMEM((TOK, LANES), BF16),
            pltpu.VMEM((SHARDS, 1, 2 * D), F32),
            pltpu.VMEM((SHARDS, 1, 2 * D), F32),
            pltpu.VMEM((PAGES + 6, 2 * D), F32),
            pltpu.VMEM((TILE, D), BF16),
            pltpu.VMEM((TILE, D), BF16),
            pltpu.VMEM((NY, 256, D), BF16),
            pltpu.VMEM((NY, 256, D), BF16),
            pltpu.VMEM((NY, 2, 16, 32, 256), BF16),
            pltpu.VMEM((NY, 16, 32, 256), BF16),
            pltpu.VMEM((4, 256, TOK), BF16),
            pltpu.VMEM((3, PAY, D), BF16),
            pltpu.VMEM((PAY, D), F32),
            pltpu.VMEM((2, PAY, HALF), BF16),
            pltpu.VMEM((2, CROSS, 2 * MAIN, WIDE), BF16),
            pltpu.VMEM((2, CROSS, 112, WIDE), BF16),
            pltpu.VMEM((2, PIECES, PAY, WIDE), BF16),
            pltpu.VMEM((2, PIECES, PAY, WIDE), BF16),
            pltpu.VMEM((112, D), F32),
            pltpu.VMEM((2, PIECES, 112, WIDE), BF16),
            pltpu.VMEM((2, PIECES, 112, WIDE), BF16),
            pltpu.VMEM((16, 32, D), F32),
            pltpu.VMEM((2, 4, 2, 32, D), BF16),
            pltpu.VMEM((2, 4, 2, 32, D), BF16),
            pltpu.VMEM((32, D), BF16),
            pltpu.VMEM((32, D), BF16),
            pltpu.SemaphoreType.DMA((SHARDS,)),
            pltpu.SemaphoreType.DMA((SHARDS,)),
            pltpu.SemaphoreType.DMA((N_SENDS,)),
            pltpu.SemaphoreType.DMA((N_SENDS,)),
            pltpu.SemaphoreType.DMA((3,)),
        ],
        compiler_params=pltpu.CompilerParams(
            collective_id=0, has_side_effects=True, vmem_limit_bytes=60 * 2**20
        ),
    )(partner, slots, jnp.transpose(masters, (1, 0, 2)), tokens, cotangent.T)
    new, hidden, input_grad, grads = pl.pallas_call(
        hand_over,
        out_shape=tuple(jax.ShapeDtypeStruct(out.shape, out.dtype) for out in outs),
        in_specs=[pl.BlockSpec(memory_space=pl.ANY)] * 4,
        out_specs=(pl.BlockSpec(memory_space=pl.ANY),) * 4,
        scratch_shapes=[pltpu.VMEM(out.shape, out.dtype) for out in outs]
        + [pltpu.SemaphoreType.DMA((4,))] * 2,
    )(*outs)
    return (
        jnp.transpose(new, (1, 0, 2)),
        hidden.T,
        input_grad,
        jnp.transpose(grads, (1, 0, 2)),
    )


def solution(mesh):
    in_specs = (P("dp", None), P("dp", "shard", None), P("dp", "shard"), P(), P())
    out_specs = (
        P("dp", "shard", None),
        P("dp", "shard"),
        P(("dp", "shard"), None),
        P("dp", "shard", None),
    )
    return jax.shard_map(body, mesh=mesh, in_specs=in_specs, out_specs=out_specs, check_vma=False)
```
